256 devices in a mesh: dp: 8 (over y, core), fsdp: 32 (over x, z).
Axes of the slice: x: 4, y: 4, z: 8, core: 2. Of those that a mesh axis runs over, the one named last changes fastest.
Arguments:
- tokens: bfloat16 [32768, 4096], P(('dp', 'fsdp')), may hold values from -18 to 18
- upstream: bfloat16 [32768, 1024], P(('dp', 'fsdp')), may hold values from -6 to 6
- weight: bfloat16 [4096, 1024], P('fsdp'), may hold values from -0.09375 to 0.09375
- owner_table: int32 [16], replicated, may hold values from 0 to 15, as said below
- stats_prev: float32 [32, 512, 512], P('fsdp'), may hold values from -589824 to 1207959552, as said below
- roots_prev: float32 [32, 512, 512], P('fsdp'), may hold values from -1 to 1.1, as said below
Outputs:
- projected: bfloat16 [32768, 1024], P(('dp', 'fsdp'))
- input_grad: bfloat16 [32768, 4096], P(('dp', 'fsdp'))
- roots_next: float32 [32, 512, 512], P('fsdp')
- direction: bfloat16 [4096, 1024], P('fsdp', 'dp')
The draws below stay inside these ranges and needn't reach their ends.
Inputs may be any that keep to these rules, and one draw needn't show every extreme that they name: `owner_table`: each of the 16 blocks appears once, and entry 0 holds block 0. `stats_prev`: each entry is symmetric and positive definite. `roots_prev`: each entry is symmetric with eigenvalues between 0.7 and 1.1.
All inputs are finite; a program needn't handle non-finite values.
Results may differ from the reference program's by a relative error of at most 0.001.
Values may be sent and summed in bfloat16 or wider, within the bound.
A program may use at most 128 MiB of HBM per device.

```python
import math
import jax
import jax.numpy as jnp
from jax import lax

D = 4096
KVW = 1024
BS = 512
HALF = 256
NB = 16
SLOTS = 1
TOKENS = 32768


def symmetric_noise(key, amount, order):
    noise = jax.random.uniform(key, (amount, order, order), jnp.float32, -1.0, 1.0)
    return 0.5 * (noise + jnp.swapaxes(noise, 1, 2))


def draw_tokens(key, part):
    key = jax.random.fold_in(key, 5)
    first_key, second_key = jax.random.split(key)
    group_scale = jnp.exp(jax.random.uniform(first_key, (D // HALF,), jnp.float32, math.log(0.3), math.log(3.0)))
    column_scale = jnp.repeat(group_scale, HALF)
    noise = jnp.clip(jax.random.normal(second_key, (TOKENS, D), jnp.float32), -6.0, 6.0)
    return (noise * column_scale[None, :]).astype(jnp.bfloat16)


def draw_owner_table(key, part):
    key = jax.random.fold_in(key, 37)
    shuffled = jax.random.permutation(key, NB).astype(jnp.int32)
    positions = jnp.arange(NB, dtype=jnp.int32)
    zero_place = jnp.sum(jnp.where(shuffled == 0, positions, 0)).astype(jnp.int32)
    first_value = shuffled[0]
    moved = jnp.where(positions == zero_place, first_value, shuffled)
    return jnp.where(positions == 0, jnp.int32(0), moved).astype(jnp.int32)


def draw_stats_prev(key, part):
    key = jax.random.fold_in(key, 11)
    first_key, second_key = jax.random.split(key)
    diagonal = jnp.exp(jax.random.uniform(first_key, (2 * NB, BS), jnp.float32, math.log(0.6), math.log(6.0)))
    root_diag = jnp.sqrt(diagonal)
    identity = jnp.eye(BS, dtype=jnp.float32)
    offdiag = 0.3 / BS * symmetric_noise(second_key, 2 * NB, BS) * root_diag[:, :, None] * root_diag[:, None, :]
    matrix = offdiag * (1.0 - identity) + identity * diagonal[:, :, None]
    return matrix * (1.0 * BS * TOKENS)


def draw_roots_prev(key, part):
    key = jax.random.fold_in(key, 23)
    first_key, second_key = jax.random.split(key)
    diagonal = jax.random.uniform(first_key, (2 * NB, BS), jnp.float32, 0.75, 1.05)
    identity = jnp.eye(BS, dtype=jnp.float32)
    offdiag = 0.05 / BS * symmetric_noise(second_key, 2 * NB, BS)
    return offdiag * (1.0 - identity) + identity * diagonal[:, :, None]


def block_scale(key, shape, pieces, least, top_value):
    loudness = 1.0
    for dim, shards_of in pieces:
        heights = jax.random.uniform(jax.random.fold_in(jax.random.fold_in(key, 6), dim), (shards_of,), jnp.float32, least / len(pieces), top_value / len(pieces))
        loudness = loudness * jnp.repeat(jnp.exp(heights), shape[dim] // shards_of).reshape((-1,) + (1,) * (len(shape) - 1 - dim))
    return loudness


def scatter_about(key, dims, scale, most, pieces=(), kind=jnp.bfloat16):
    drawn = scale * jax.random.normal(key, dims, jnp.float32)
    if pieces:
        drawn = drawn * block_scale(key, dims, pieces, -0.22, 0.18)
    return jnp.clip(drawn, -most, most).astype(kind)


def setup_inputs(seed: int = 0) -> dict:
    seeds = jax.random.split(jax.random.key(seed), 7)
    return {
        "tokens": draw_tokens(jax.random.fold_in(seeds[6], 71), 0),
        "upstream": scatter_about(seeds[1], (TOKENS, KVW), 1.0, 6.0, ((0, 256),)),
        "weight": scatter_about(seeds[2], (D, KVW), D ** -0.5, 0.09375, ((0, 32),)),
        "owner_table": draw_owner_table(jax.random.fold_in(seeds[6], 71), 0),
        "stats_prev": draw_stats_prev(jax.random.fold_in(seeds[6], 71), 0),
        "roots_prev": draw_roots_prev(jax.random.fold_in(seeds[6], 71), 0),
    }


HIGHEST = lax.Precision.HIGHEST
STAT_DECAY = 0.8
NORM_EPSILON = 1e-06

def matmul(left, right):
    return jnp.dot(left, right, precision=HIGHEST)

def block_of(gradient, chosen):
    col_blocks = KVW // BS
    row_first = (chosen // col_blocks * BS).astype(jnp.int32)
    col_first = (chosen % col_blocks * BS).astype(jnp.int32)
    return (lax.dynamic_slice(gradient, (row_first, col_first), (BS, BS)), row_first, col_first)

def reference(tokens, upstream, weight, owner_table, stats_prev, roots_prev):
    projected = jnp.dot(tokens, weight, preferred_element_type=jnp.float32).astype(jnp.bfloat16)
    input_grad = lax.dot_general(upstream, weight, (((1,), (1,)), ((), ())), preferred_element_type=jnp.float32).astype(jnp.bfloat16)
    gradient = lax.dot_general(tokens, upstream, (((0,), (0,)), ((), ())), preferred_element_type=jnp.float32)
    identity = jnp.eye(BS, dtype=jnp.float32)
    roots_list = []
    for entry in range(2 * NB):
        group = entry // (2 * SLOTS)
        side_bit = entry // SLOTS % 2
        slot_index = entry % SLOTS
        chosen = owner_table[group * SLOTS + slot_index]
        grad_block, row_first, col_first = block_of(gradient, chosen)
        picked = grad_block if side_bit == 0 else grad_block.T
        gram_matrix = matmul(picked, picked.T)
        stats = STAT_DECAY * stats_prev[entry] + (1.0 - STAT_DECAY) * gram_matrix
        normed = stats / (jnp.trace(stats) / BS)
        start_root = roots_prev[entry]
        square = matmul(start_root, start_root)
        moment = matmul(matmul(square, square), normed)
        factor = (5.0 * identity - moment) * 0.25
        iterate = matmul(start_root, factor)
        factor_sq = matmul(factor, factor)
        moment = matmul(matmul(factor_sq, factor_sq), moment)
        factor = (5.0 * identity - moment) * 0.25
        roots_list.append(matmul(iterate, factor))
    direction = jnp.zeros((D, KVW), jnp.bfloat16)
    for place in range(NB):
        group = place // SLOTS
        slot_index = place % SLOTS
        left_root = roots_list[group * 2 * SLOTS + slot_index]
        right_root = roots_list[group * 2 * SLOTS + SLOTS + slot_index]
        grad_block, row_first, col_first = block_of(gradient, owner_table[place])
        product = matmul(matmul(left_root, grad_block), right_root)
        norm_value = jnp.sqrt(jnp.mean(product * product) + NORM_EPSILON)
        direction = lax.dynamic_update_slice(direction, (product / norm_value).astype(jnp.bfloat16), (row_first, col_first))
    return (projected, input_grad, jnp.stack(roots_list), direction)
```

```python
import functools

import jax
import jax.numpy as jnp
from jax import lax
from jax.experimental import pallas as pl
from jax.experimental.pallas import tpu as pltpu
from jax.sharding import PartitionSpec as P

HIGH = lax.Precision.HIGH
STAT_DECAY = 0.8
NORM_EPSILON = 1e-06
MESH = pl.DeviceIdType.MESH
VMEM_LIMIT = 48 * 1024 * 1024

NX, NY, NZ = 4, 4, 8
BS = 512
ROWS = 128
COLS = 256
HALF = 64
NB = 16


def remote(src, dst, send, recv, dp, fsdp):
    return pltpu.make_async_remote_copy(
        src_ref=src,
        dst_ref=dst,
        send_sem=send,
        recv_sem=recv,
        device_id=(dp, fsdp),
        device_id_type=MESH,
    )


def greet(peers):
    barrier = pltpu.get_barrier_semaphore()
    for dp, fsdp in peers:
        pl.semaphore_signal(barrier, inc=1, device_id=(dp, fsdp), device_id_type=MESH)
    pl.semaphore_wait(barrier, len(peers))


def lanes(start, size):
    return pl.ds(pl.multiple_of(start, 128), size)


def pool_kernel(tok, ups, tok_out, ups_out, t_send, t_recv, f_send, f_recv, u_send, u_recv, own):
    me, fs = lax.axis_index("dp"), lax.axis_index("fsdp")
    y, core = me // 2, me % 2
    sibling = y * 2 + 1 - core
    greet([(lax.rem(me + d, 8), fs) for d in range(1, 8)])

    def token_parts(to_y, where):
        for r in range(8):
            yield tok.at[:, lanes(512 * r + 128 * to_y, 128)], where.at[me, :, pl.ds(128 * r, 128)]

    def upstream_parts(to_core):
        for b in range(2):
            yield ups.at[:, lanes(512 * b + 256 * to_core, 256)], ups_out.at[b, me]

    for d in (1, 3, 2):
        to_y = lax.rem(y + d, 4)
        for src, dst in token_parts(to_y, tok_out):
            remote(src, dst, t_send.at[d], t_recv.at[d], to_y * 2 + core, fs).start()
    for src, dst in token_parts(y, tok_out):
        remote(src, dst, f_send.at[0], f_recv.at[0], sibling, fs).start()
    for d in (1, 3, 2, 0):
        to_y = lax.rem(y + d, 4)
        for flip in range(2):
            if d == 0 and flip == 0:
                continue
            to_core = core if flip == 0 else 1 - core
            for src, dst in upstream_parts(to_core):
                k = 2 * d + flip
                remote(src, dst, u_send.at[k], u_recv.at[k], to_y * 2 + to_core, fs).start()
    for src, dst in token_parts(y, tok_out):
        pltpu.make_async_copy(src, dst, own.at[0]).start()
    for src, dst in upstream_parts(core):
        pltpu.make_async_copy(src, dst, own.at[1]).start()

    def whole(send, recv, buf, slot):
        return remote(buf.at[slot], buf.at[slot], send, recv, sibling, fs)

    def both(send, recv, slot):
        return remote(ups_out.at[:, slot], ups_out.at[:, slot], send, recv, sibling, fs)

    for d in (1, 3, 2):
        slot = lax.rem(y + 4 - d, 4) * 2 + core
        whole(t_send.at[d], t_recv.at[d], tok_out, slot).wait_recv()
        whole(f_send.at[d], f_recv.at[d], tok_out, slot).start()
    for d in range(4):
        slot = lax.rem(y + 4 - d, 4) * 2 + 1 - core
        whole(f_send.at[d], f_recv.at[d], tok_out, slot).wait()
        if d:
            whole(t_send.at[d], t_recv.at[d], tok_out, slot).wait_send()
    for d in range(4):
        for flip in range(2):
            if d == 0 and flip == 0:
                continue
            from_core = core if flip == 0 else 1 - core
            slot = lax.rem(y + 4 - d, 4) * 2 + from_core
            k = 2 * d + flip
            both(u_send.at[k], u_recv.at[k], slot).wait()
    pltpu.make_async_copy(tok_out.at[me], tok_out.at[me], own.at[0]).wait()
    pltpu.make_async_copy(ups_out.at[:, me], ups_out.at[:, me], own.at[1]).wait()


def pool(tokens, upstream):
    rows = tokens.shape[0]
    dma = pltpu.SemaphoreType.DMA
    return pl.pallas_call(
        pool_kernel,
        out_shape=(
            jax.ShapeDtypeStruct((8, rows, 1024), jnp.bfloat16),
            jax.ShapeDtypeStruct((2, 8, rows, 256), jnp.bfloat16),
        ),
        in_specs=[pl.BlockSpec(memory_space=pl.ANY)] * 2,
        out_specs=(pl.BlockSpec(memory_space=pl.ANY),) * 2,
        scratch_shapes=[dma((4,)), dma((4,)), dma((4,)), dma((4,)), dma((8,)), dma((8,)), dma((2,))],
        compiler_params=pltpu.CompilerParams(
            collective_id=0, has_side_effects=True, vmem_limit_bytes=VMEM_LIMIT
        ),
        cost_estimate=pl.CostEstimate(flops=0, bytes_accessed=64 << 20, transcendentals=0),
    )(tokens, upstream)


def sum_kernel(
    table, part0, part1, block, outgoing, xbuf, xsum, zbuf, x_send, x_recv, z_send, z_recv, g_send, g_recv, f_send, f_recv
):
    me, fs = lax.axis_index("dp"), lax.axis_index("fsdp")
    y, core, x, z = me // 2, me % 2, fs // 8, fs % 8
    side = z % 2
    sibling = y * 2 + 1 - core
    mate = x * 8 + z + 1 - 2 * side

    peers = [(me, lax.rem(x + d, 4) * 8 + z) for d in range(1, 4)]
    peers += [(me, x * 8 + lax.rem(z + d, 8)) for d in range(1, 8)]
    peers += [(lax.rem(y + d, 4) * 2 + core, fs) for d in range(1, 4)]
    peers += [(lax.rem(y + d, 4) * 2 + core, mate) for d in range(1, 4)]
    peers += [(sibling, fs)]
    greet(peers)

    def arrange(x_to):
        def body(i, _):
            g = x_to * 4 + i
            chosen = table[g]
            band = lax.div(chosen, 2)
            piece = jnp.where(lax.rem(chosen, 2) == 0, part0[band], part1[band])
            outgoing[2 * g] = piece[:HALF]
            outgoing[2 * g + 1] = piece[HALF:]
            return 0

        lax.fori_loop(0, 4, body, 0)

    def x_copy(d):
        to = lax.rem(x + d, 4)
        return remote(
            outgoing.at[pl.ds(to * 8, 8)], xbuf.at[d], x_send.at[d], x_recv.at[d], me, to * 8 + z
        )

    for d in (2, 1, 3, 0):
        arrange(lax.rem(x + d, 4))
        if d:
            x_copy(d).start()
    for d in (1, 3, 2):
        x_copy(d).wait_recv()

    def z_copy(d):
        to = lax.rem(z + d, 8)
        return remote(xsum.at[to], zbuf.at[d], z_send.at[d], z_recv.at[d], me, x * 8 + to)

    for d in (4, 3, 5, 2, 6, 1, 7, 0):
        to = lax.rem(z + d, 8)
        xsum[to] = (outgoing[x * 8 + to] + xbuf[1, to]) + (xbuf[2, to] + xbuf[3, to])
        if d:
            z_copy(d).start()
    total = xsum[z]
    for d in (1, 7, 2, 6, 3, 5, 4):
        z_copy(d).wait_recv()
        total = total + zbuf[d]

    def place(of_y, of_side, of_core):
        return block.at[pl.ds(pl.multiple_of(of_y * ROWS + of_side * HALF, HALF), HALF), lanes(of_core * COLS, COLS)]

    own = place(y, side, core)
    own[...] = total

    def g_copy(d, flip, spot):
        fs_to = mate if flip else fs
        k = 2 * d + flip
        return remote(spot, spot, g_send.at[k], g_recv.at[k], lax.rem(y + d, 4) * 2 + core, fs_to)

    order = [(d, flip) for d in (2, 1, 3, 0) for flip in range(2) if d or flip]
    for d, flip in order:
        g_copy(d, flip, own).start()

    def f_copy(k, spot):
        return remote(spot, spot, f_send.at[k], f_recv.at[k], sibling, fs)

    f_copy(0, own).start()
    for d, flip in reversed(order):
        spot = place(lax.rem(y + 4 - d, 4), 1 - side if flip else side, core)
        g_copy(d, flip, spot).wait_recv()
        f_copy(2 * d + flip, spot).start()
    for d in range(4):
        for flip in range(2):
            spot = place(lax.rem(y + 4 - d, 4), 1 - side if flip else side, 1 - core)
            f_copy(2 * d + flip, spot).wait()
    for d in (1, 2, 3):
        x_copy(d).wait_send()
    for d in range(1, 8):
        z_copy(d).wait_send()
    for d, flip in order:
        g_copy(d, flip, own).wait_send()


def sum_blocks(table, parts):
    dma = pltpu.SemaphoreType.DMA
    f32 = jnp.float32
    return pl.pallas_call(
        sum_kernel,
        out_shape=jax.ShapeDtypeStruct((BS, BS), f32),
        in_specs=[pl.BlockSpec(memory_space=pltpu.SMEM)] + [pl.BlockSpec(memory_space=pltpu.VMEM)] * 2,
        out_specs=pl.BlockSpec(memory_space=pltpu.VMEM),
        scratch_shapes=[
            pltpu.VMEM((32, HALF, COLS), f32),
            pltpu.VMEM((4, 8, HALF, COLS), f32),
            pltpu.VMEM((8, HALF, COLS), f32),
            pltpu.VMEM((8, HALF, COLS), f32),
        ]
        + [dma((4,)), dma((4,))]
        + [dma((8,))] * 6,
        compiler_params=pltpu.CompilerParams(
            collective_id=1, has_side_effects=True, vmem_limit_bytes=VMEM_LIMIT
        ),
        cost_estimate=pl.CostEstimate(flops=0, bytes_accessed=64 << 20, transcendentals=0),
    )(table, *parts)


def finish_kernel(
    inverse, left_rows, root, out, rows_in, energies, chunks, spread, picked,
    a_send, a_recv, e_send, e_recv, s_send, s_recv, p_send, p_recv, local
):
    me, fs = lax.axis_index("dp"), lax.axis_index("fsdp")
    z = fs % 8
    group, side = fs // 2, z % 2
    piece = z % 4
    sources = [(2 * piece + i, 2 * (4 * q + me % 4) + 1, i, q) for i in range(2) for q in range(4)]
    my_piece, my_quarter, my_cols = me // 2, group // 4, group % 4
    places = [
        (4 * cb + my_cols, 4 * rb + my_piece, 2 * rb + cb) for rb in range(8) for cb in range(2)
    ]
    barrier = pltpu.get_barrier_semaphore()

    def tell(dp, fsdp):
        pl.semaphore_signal(barrier, inc=1, device_id=(dp, fsdp), device_id_type=MESH)

    for dp, fsdp, _, _ in sources:
        @pl.when(jnp.logical_or(dp != me, fsdp != fs))
        def _(dp=dp, fsdp=fsdp):
            tell(dp, fsdp)

    def out_rows(i, q):
        return out.at[pl.ds(pl.multiple_of(HALF * i + 16 * q, 16), 16)]

    def a_copy():
        return remote(left_rows, rows_in, a_send, a_recv, me, fs + 1 - 2 * side)

    @pl.when(side == 0)
    def _():
        pl.semaphore_wait(barrier, 1)
        a_copy().start()
        a_copy().wait_send()

    @pl.when(side == 1)
    def _():
        tell(me, fs - 1)
        for d in range(1, 8):
            tell(lax.rem(me + d, 8), fs)
        for d in range(1, NB):
            tell(me, lax.rem(fs + 2 * d, 32))
        is_own = jnp.int32(0)
        for dp, fsdp, _ in places:
            is_own += jnp.where(jnp.logical_and(dp == me, fsdp == fs), 1, 0)
        pl.semaphore_wait(barrier, 7 + 15 + 16 - is_own)

        a_copy().wait_recv()
        product = jnp.dot(
            rows_in[...], root[...], precision=lax.Precision.HIGHEST, preferred_element_type=jnp.float32
        )
        energy = jnp.sum(product * product)
        energies[0] = jnp.full((8, 128), energy, jnp.float32)

        def e_copy(d):
            return remote(
                energies.at[0], energies.at[d], e_send.at[d], e_recv.at[d], lax.rem(me + d, 8), fs
            )

        for d in range(1, 8):
            e_copy(d).start()
        for d in range(1, 8):
            e_copy(d).wait_recv()

        total = jnp.zeros((8, 128), jnp.float32)
        for dp in range(8):
            total = total + energies[lax.rem(me - dp + 8, 8)]
        mean = total[0:1, 0:1] / (BS * BS)
        update = (product / jnp.sqrt(mean + NORM_EPSILON)).astype(jnp.bfloat16)
        for j in range(NB):
            q, k = j // 4, j % 4
            chunks[j] = update[16 * q : 16 * q + 16, 128 * k : 128 * k + 128]

        def s_copy(d):
            to = lax.rem(group + d, NB)
            return remote(
                chunks.at[to], spread.at[group], s_send.at[d], s_recv.at[d], me, 2 * to + 1
            )

        for d in range(1, NB):
            s_copy(d).start()
        spread[group] = chunks[group]
        for d in range(1, NB):
            source = lax.rem(group + NB - d, NB)
            remote(
                chunks.at[0], spread.at[source], s_send.at[d], s_recv.at[d], me, 2 * source + 1
            ).wait_recv()
        for dp, fsdp, b in places:
            picked[b] = spread[inverse[b]]

        def p_copy(dp, fsdp, b):
            i, q = me % 2, my_quarter
            return remote(picked.at[b], out_rows(i, q), p_send.at[b], p_recv.at[4 * i + q], dp, fsdp)

        for dp, fsdp, b in places:
            mine = jnp.logical_and(dp == me, fsdp == fs)

            @pl.when(mine)
            def _(b=b):
                copy = pltpu.make_async_copy(picked.at[b], out_rows(me % 2, my_quarter), local)
                copy.start()
                copy.wait()

            @pl.when(jnp.logical_not(mine))
            def _(dp=dp, fsdp=fsdp, b=b):
                p_copy(dp, fsdp, b).start()

        for d in range(1, 8):
            e_copy(d).wait_send()
        for d in range(1, NB):
            s_copy(d).wait_send()
        for dp, fsdp, b in places:
            @pl.when(jnp.logical_or(dp != me, fsdp != fs))
            def _(dp=dp, fsdp=fsdp, b=b):
                p_copy(dp, fsdp, b).wait_send()

    for dp, fsdp, i, q in sources:
        @pl.when(jnp.logical_or(dp != me, fsdp != fs))
        def _(dp=dp, fsdp=fsdp, i=i, q=q):
            remote(picked.at[0], out_rows(i, q), p_send.at[0], p_recv.at[4 * i + q], dp, fsdp).wait_recv()


def finish(inverse, left_rows, root):
    dma = pltpu.SemaphoreType.DMA
    f32, b16 = jnp.float32, jnp.bfloat16
    vmem = pl.BlockSpec(memory_space=pltpu.VMEM)
    return pl.pallas_call(
        finish_kernel,
        out_shape=jax.ShapeDtypeStruct((128, 128), b16),
        in_specs=[pl.BlockSpec(memory_space=pltpu.SMEM), vmem, vmem],
        out_specs=vmem,
        scratch_shapes=[
            pltpu.VMEM((HALF, BS), f32),
            pltpu.VMEM((8, 8, 128), f32),
            pltpu.VMEM((NB, 16, 128), b16),
            pltpu.VMEM((NB, 16, 128), b16),
            pltpu.VMEM((NB, 16, 128), b16),
            dma(()),
            dma(()),
            dma((8,)),
            dma((8,)),
            dma((NB,)),
            dma((NB,)),
            dma((NB,)),
            dma((8,)),
            dma(()),
        ],
        compiler_params=pltpu.CompilerParams(
            collective_id=2, has_side_effects=True, vmem_limit_bytes=VMEM_LIMIT
        ),
        cost_estimate=pl.CostEstimate(flops=0, bytes_accessed=32 << 20, transcendentals=0),
    )(inverse, left_rows, root)


def mm(left, right):
    return jnp.dot(left, right, precision=HIGH, preferred_element_type=jnp.float32)


def newton(grad_block, stats_prev, root_prev, is_left):
    chosen = jnp.where(is_left, grad_block, grad_block.T)
    gram = mm(chosen, chosen.T)
    stats = STAT_DECAY * stats_prev + (1.0 - STAT_DECAY) * gram
    normed = stats / (jnp.trace(stats) / BS)
    identity = jnp.eye(BS, dtype=jnp.float32)
    square = mm(root_prev, root_prev)
    moment = mm(mm(square, square), normed)
    factor = (5.0 * identity - moment) * 0.25
    iterate = mm(root_prev, factor)
    factor_sq = mm(factor, factor)
    moment = mm(mm(factor_sq, factor_sq), moment)
    factor = (5.0 * identity - moment) * 0.25
    return mm(iterate, factor)


def local(tokens, upstream, weight, owner_table, stats_prev, roots_prev):
    dp, fs = lax.axis_index("dp"), lax.axis_index("fsdp")
    full_weight = lax.all_gather(weight, "fsdp", axis=0, tiled=True)

    tok_pool, ups_pool = pool(tokens, upstream)
    parts = [
        lax.dot_general(
            tok_pool.reshape(-1, 1024),
            ups_pool[b].reshape(-1, COLS),
            (((0,), (0,)), ((), ())),
            preferred_element_type=jnp.float32,
        ).reshape(8, ROWS, COLS)
        for b in range(2)
    ]
    grad_block = sum_blocks(owner_table, parts)
    is_left = fs % 2 == 0
    root = newton(grad_block, stats_prev[0], roots_prev[0], is_left)
    left_rows = mm(lax.dynamic_slice_in_dim(root, dp * HALF, HALF, 0), grad_block)
    positions = jnp.arange(NB, dtype=jnp.int32)
    inverse = jnp.sum(
        jnp.where(owner_table[None, :] == positions[:, None], positions[None, :], 0), axis=1
    )
    direction = finish(inverse, left_rows, root)

    tokens, upstream, direction = lax.optimization_barrier((tokens, upstream, direction))
    projected = jnp.dot(tokens, full_weight, preferred_element_type=jnp.float32).astype(jnp.bfloat16)
    input_grad = lax.dot_general(
        upstream, full_weight, (((1,), (1,)), ((), ())), preferred_element_type=jnp.float32
    ).astype(jnp.bfloat16)
    return projected, input_grad, root[None], direction


def solution(mesh):
    placed = (
        P(("dp", "fsdp"), None),
        P(("dp", "fsdp"), None),
        P("fsdp", None),
        P(),
        P("fsdp", None, None),
        P("fsdp", None, None),
    )
    return jax.shard_map(
        local,
        mesh=mesh,
        in_specs=placed,
        out_specs=(
            P(("dp", "fsdp"), None),
            P(("dp", "fsdp"), None),
            P("fsdp", None, None),
            P("fsdp", "dp"),
        ),
        check_vma=False,
    )
```

```python
import functools

import jax
import jax.numpy as jnp
from jax import lax
from jax.experimental import pallas as pl
from jax.experimental.pallas import tpu as pltpu
from jax.sharding import PartitionSpec as P

HIGH = lax.Precision.HIGH
STAT_DECAY = 0.8
NORM_EPSILON = 1e-06
MESH = pl.DeviceIdType.MESH
VMEM_LIMIT = 48 * 1024 * 1024

NX, NY, NZ = 4, 4, 8
BS = 512
ROWS = 128
COLS = 256
HALF = 64
NB = 16
RA = 48
WA = 768


def remote(src, dst, send, recv, dp, fsdp):
    return pltpu.make_async_remote_copy(
        src_ref=src,
        dst_ref=dst,
        send_sem=send,
        recv_sem=recv,
        device_id=(dp, fsdp),
        device_id_type=MESH,
    )


def greet(peers):
    barrier = pltpu.get_barrier_semaphore()
    for dp, fsdp in peers:
        pl.semaphore_signal(barrier, inc=1, device_id=(dp, fsdp), device_id_type=MESH)
    pl.semaphore_wait(barrier, len(peers))


def lanes(start, size):
    return pl.ds(pl.multiple_of(start, 128), size)


def gradient_kernel(
    table, tok, ups, shard, block, weight,
    tok_in, tok_t, ups_in, part, outgoing, xa_in, za_sum, za_in, zb_in, xb_sum, xb_in,
    t_send, t_recv, f_send, f_recv, u_send, u_recv,
    xa_send, xa_recv, za_send, za_recv, zb_send, zb_recv, xb_send, xb_recv,
    g_send, g_recv, h_send, h_recv,
    wza_send, wza_recv, wxa_send, wxa_recv, wzb_send, wzb_recv, wxb_send, wxb_recv,
    wy_send, wy_recv, wc_send, wc_recv, own,
):
    me, fs = lax.axis_index("dp"), lax.axis_index("fsdp")
    y, core, x, z = me // 2, me % 2, fs // 8, fs % 8
    side = z % 2
    sibling = y * 2 + 1 - core
    mate = x * 8 + z + 1 - 2 * side

    def to_x(d):
        return lax.rem(x + d, 4)

    def to_y(d):
        return lax.rem(y + d, 4)

    def to_z(d):
        return lax.rem(z + d, 8)

    peers = [(lax.rem(me + d, 8), fs) for d in range(1, 8)]
    peers += [(me, to_x(d) * 8 + z) for d in range(1, 4)]
    peers += [(me, x * 8 + to_z(d)) for d in range(1, 8)]
    peers += [(to_y(d) * 2 + core, mate) for d in range(1, 4)]
    greet(peers)

    def token_parts(of_y, where):
        for r in range(8):
            yield tok.at[:, lanes(512 * r + 128 * of_y, 128)], where.at[me, :, pl.ds(128 * r, 128)]

    def upstream_parts(of_core):
        for b in range(2):
            yield ups.at[:, lanes(512 * b + 256 * of_core, 256)], ups_in.at[b, me]

    for d in (2, 1, 3):
        for src, dst in token_parts(to_y(d), tok_in):
            remote(src, dst, t_send.at[d], t_recv.at[d], to_y(d) * 2 + core, fs).start()
    for src, dst in token_parts(y, tok_in):
        remote(src, dst, f_send.at[0], f_recv.at[0], sibling, fs).start()

    own_rows = pl.ds(pl.multiple_of(64 * (y % 2) + 32 * core, 32), 32)
    other_rows = pl.ds(pl.multiple_of(64 * (1 - y % 2) + 32 * core, 32), 32)
    ca, cb = pl.ds(0, WA), pl.ds(WA, 1024 - WA)

    def wza(d):
        return remote(
            shard.at[own_rows, ca], weight.at[x, z, own_rows, ca],
            wza_send.at[d], wza_recv.at[d], me, x * 8 + to_z(d),
        )

    def wxb(d):
        return remote(
            shard.at[own_rows, cb], weight.at[x, z, own_rows, cb],
            wxb_send.at[d], wxb_recv.at[d], me, to_x(d) * 8 + z,
        )

    def wxa(d):
        slab = weight.at[x, :, own_rows, ca]
        return remote(slab, slab, wxa_send.at[d], wxa_recv.at[d], me, to_x(d) * 8 + z)

    def wzb(d):
        slab = weight.at[:, z, own_rows, cb]
        return remote(slab, slab, wzb_send.at[d], wzb_recv.at[d], me, x * 8 + to_z(d))

    def wza_in(d):
        spot = weight.at[x, lax.rem(z + 8 - d, 8), own_rows, ca]
        return remote(spot, spot, wza_send.at[d], wza_recv.at[d], me, mate)

    def wxb_in(d):
        spot = weight.at[lax.rem(x + 4 - d, 4), z, own_rows, cb]
        return remote(spot, spot, wxb_send.at[d], wxb_recv.at[d], me, mate)

    def wxa_in(d):
        spot = weight.at[lax.rem(x + 4 - d, 4), :, own_rows, ca]
        return remote(spot, spot, wxa_send.at[d], wxa_recv.at[d], me, mate)

    def wzb_in(d):
        spot = weight.at[:, lax.rem(z + 8 - d, 8), own_rows, cb]
        return remote(spot, spot, wzb_send.at[d], wzb_recv.at[d], me, mate)

    own_shard = pltpu.make_async_copy(shard.at[own_rows], weight.at[x, z, own_rows], own.at[2])
    own_shard.start()
    for d in (4, 3, 5, 2, 6, 1, 7):
        wza(d).start()
    for d in (2, 1, 3):
        wxb(d).start()

    for d in (2, 1, 3, 0):
        for flip in range(2):
            if d == 0 and flip == 0:
                continue
            of_core = core if flip == 0 else 1 - core
            for src, dst in upstream_parts(of_core):
                k = 2 * d + flip
                remote(src, dst, u_send.at[k], u_recv.at[k], to_y(d) * 2 + of_core, fs).start()
    for src, dst in token_parts(y, tok_in):
        pltpu.make_async_copy(src, dst, own.at[0]).start()
    for src, dst in upstream_parts(core):
        pltpu.make_async_copy(src, dst, own.at[1]).start()

    def whole(send, recv, slot):
        return remote(tok_in.at[slot], tok_in.at[slot], send, recv, sibling, fs)

    def turn(slot):
        tok_t[:, lanes(slot * 128, 128)] = tok_in[slot].T

    pltpu.make_async_copy(tok_in.at[me], tok_in.at[me], own.at[0]).wait()
    turn(me)
    whole(f_send.at[0], f_recv.at[0], sibling).wait_recv()
    turn(sibling)

    own_shard.wait()
    for d in (1, 3, 2):
        wxb_in(d).wait_recv()
    for d in (4, 3, 5, 2, 6, 1, 7):
        wzb(d).start()
    for d in (1, 7, 2, 6, 3, 5, 4):
        wza_in(d).wait_recv()
    for d in (2, 1, 3):
        wxa(d).start()

    for d in (1, 3, 2):
        slot = lax.rem(y + 4 - d, 4) * 2 + core
        whole(t_send.at[d], t_recv.at[d], slot).wait_recv()
        whole(f_send.at[d], f_recv.at[d], slot).start()
        turn(slot)
    for d in (1, 3, 2):
        slot = lax.rem(y + 4 - d, 4) * 2 + 1 - core
        whole(f_send.at[d], f_recv.at[d], slot).wait_recv()
        turn(slot)
    for d in (0, 1, 3, 2):
        for flip in range(2):
            if d == 0 and flip == 0:
                continue
            from_core = core if flip == 0 else 1 - core
            slot = lax.rem(y + 4 - d, 4) * 2 + from_core
            k = 2 * d + flip
            spot = ups_in.at[:, slot]
            remote(spot, spot, u_send.at[k], u_recv.at[k], sibling, fs).wait()
    pltpu.make_async_copy(ups_in.at[:, me], ups_in.at[:, me], own.at[1]).wait()

    def multiply(i, _):
        rows = tok_t[pl.ds(pl.multiple_of(i * 256, 256), 256), :]
        for b in range(2):
            piece = jnp.dot(
                rows, ups_in[b].reshape(1024, COLS), preferred_element_type=jnp.float32
            )
            part[b, 2 * i] = piece[:ROWS]
            part[b, 2 * i + 1] = piece[ROWS:]
        return 0

    lax.fori_loop(0, 4, multiply, 0)

    def arrange(of_x):
        def body(i, _):
            chosen = table[of_x * 4 + i]
            band = lax.div(chosen, 2)
            piece = jnp.where(lax.rem(chosen, 2) == 0, part[0, band], part[1, band])
            outgoing[of_x, 2 * i] = piece[:HALF]
            outgoing[of_x, 2 * i + 1] = piece[HALF:]
            return 0

        lax.fori_loop(0, 4, body, 0)

    rows_a, rows_b = pl.ds(0, RA), pl.ds(RA, HALF - RA)

    def xa(d):
        return remote(
            outgoing.at[to_x(d), :, rows_a], xa_in.at[d], xa_send.at[d], xa_recv.at[d], me, to_x(d) * 8 + z
        )

    def zb(d):
        return remote(
            outgoing.at[:, to_z(d), rows_b], zb_in.at[d], zb_send.at[d], zb_recv.at[d], me, x * 8 + to_z(d)
        )

    def za(d):
        return remote(za_sum.at[to_z(d)], za_in.at[d], za_send.at[d], za_recv.at[d], me, x * 8 + to_z(d))

    def xb(d):
        return remote(xb_sum.at[to_x(d)], xb_in.at[d], xb_send.at[d], xb_recv.at[d], me, to_x(d) * 8 + z)

    for d in (2, 1, 3, 0):
        arrange(to_x(d))
        if d:
            xa(d).start()
    for d in (4, 3, 5, 2, 6, 1, 7):
        zb(d).start()

    for d in (1, 3, 2):
        wxa_in(d).wait_recv()
    for d in (1, 7, 2, 6, 3, 5, 4):
        wzb_in(d).wait_recv()

    def wy(d):
        slab = weight.at[pl.ds(0 if d == 1 else 2, 2), :, own_rows]
        return remote(slab, slab, wy_send.at[d], wy_recv.at[d], to_y(d) * 2 + core, fs)

    def wy_in(d):
        return weight.at[pl.ds(0 if d == 1 else 2, 2), :, other_rows]

    def wc(k, spot):
        return remote(spot, spot, wc_send.at[k], wc_recv.at[k], sibling, fs)

    wy(1).start()
    wy(3).start()
    wc(0, weight.at[:, :, own_rows]).start()

    for d in (1, 7, 2, 6, 3, 5, 4):
        zb(d).wait_recv()
    for d in (2, 1, 3, 0):
        to = to_x(d)
        total = outgoing[to, z, RA:]
        for k in range(1, 8):
            total = total + zb_in[k, to]
        xb_sum[to] = total
        if d:
            xb(d).start()
    for d in (1, 3, 2):
        xa(d).wait_recv()
    for d in (4, 3, 5, 2, 6, 1, 7, 0):
        to = to_z(d)
        za_sum[to] = (outgoing[x, to, :RA] + xa_in[1, to]) + (xa_in[2, to] + xa_in[3, to])
        if d:
            za(d).start()

    def place(of_y, of_side, of_core):
        return block.at[
            pl.ds(pl.multiple_of(of_y * ROWS + of_side * HALF, HALF), HALF), lanes(of_core * COLS, COLS)
        ]

    mine = place(y, side, core)
    total = xb_sum[x]
    for d in (1, 3, 2):
        xb(d).wait_recv()
        total = total + xb_in[d]
    mine[rows_b] = total
    total = za_sum[z]
    for d in (1, 7, 2, 6, 3, 5, 4):
        za(d).wait_recv()
        total = total + za_in[d]
    mine[rows_a] = total

    def g_copy(d, flip, spot):
        k = 2 * d + flip
        return remote(spot, spot, g_send.at[k], g_recv.at[k], to_y(d) * 2 + core, mate if flip else fs)

    def h_copy(k, spot):
        return remote(spot, spot, h_send.at[k], h_recv.at[k], sibling, fs)

    order = [(d, flip) for d in (2, 1, 3, 0) for flip in range(2) if d or flip]
    for d, flip in order:
        g_copy(d, flip, mine).start()
    h_copy(0, mine).start()
    for d, flip in reversed(order):
        spot = place(lax.rem(y + 4 - d, 4), 1 - side if flip else side, core)
        g_copy(d, flip, spot).wait_recv()
        h_copy(2 * d + flip, spot).start()

    for d in (1, 3):
        remote(wy_in(d), wy_in(d), wy_send.at[d], wy_recv.at[d], sibling, fs).wait_recv()
        wc(d, wy_in(d)).start()

    for d in range(4):
        for flip in range(2):
            spot = place(lax.rem(y + 4 - d, 4), 1 - side if flip else side, 1 - core)
            h_copy(2 * d + flip, spot).wait()

    sib_rows = pl.ds(pl.multiple_of(64 * (y % 2) + 32 * (1 - core), 32), 32)
    sib_other = pl.ds(pl.multiple_of(64 * (1 - y % 2) + 32 * (1 - core), 32), 32)
    wc(0, weight.at[:, :, sib_rows]).wait()
    for d in (1, 3):
        wc(d, weight.at[pl.ds(0 if d == 1 else 2, 2), :, sib_other]).wait()

    for d in range(1, 4):
        whole(t_send.at[d], t_recv.at[d], me).wait_send()
        xa(d).wait_send()
        xb(d).wait_send()
        wxa(d).wait_send()
        wxb(d).wait_send()
    for d in range(4):
        whole(f_send.at[d], f_recv.at[d], me).wait_send()
    for d in range(1, 8):
        za(d).wait_send()
        zb(d).wait_send()
        wza(d).wait_send()
        wzb(d).wait_send()
    for d, flip in order:
        g_copy(d, flip, mine).wait_send()
    wy(1).wait_send()
    wy(3).wait_send()


def gradient_blocks(table, tokens, upstream, shard):
    dma = pltpu.SemaphoreType.DMA
    f32, b16 = jnp.float32, jnp.bfloat16
    anywhere = pl.BlockSpec(memory_space=pl.ANY)
    rows = tokens.shape[0]
    return pl.pallas_call(
        gradient_kernel,
        out_shape=(
            jax.ShapeDtypeStruct((BS, BS), f32),
            jax.ShapeDtypeStruct((NX, NZ, 128, 1024), b16),
        ),
        in_specs=[pl.BlockSpec(memory_space=pltpu.SMEM), anywhere, anywhere, anywhere],
        out_specs=(pl.BlockSpec(memory_space=pltpu.VMEM), anywhere),
        scratch_shapes=[
            pltpu.VMEM((8, rows, 1024), b16),
            pltpu.VMEM((1024, 8 * rows), b16),
            pltpu.VMEM((2, 8, rows, COLS), b16),
            pltpu.VMEM((2, 8, ROWS, COLS), f32),
            pltpu.VMEM((NX, NZ, HALF, COLS), f32),
            pltpu.VMEM((NX, NZ, RA, COLS), f32),
            pltpu.VMEM((NZ, RA, COLS), f32),
            pltpu.VMEM((NZ, RA, COLS), f32),
            pltpu.VMEM((NZ, NX, HALF - RA, COLS), f32),
            pltpu.VMEM((NX, HALF - RA, COLS), f32),
            pltpu.VMEM((NX, HALF - RA, COLS), f32),
        ]
        + [dma((4,))] * 4
        + [dma((8,))] * 2
        + [dma((4,))] * 2
        + [dma((8,))] * 4
        + [dma((4,))] * 2
        + [dma((8,))] * 4
        + [dma((8,))] * 2
        + [dma((4,))] * 2
        + [dma((8,))] * 2
        + [dma((4,))] * 6
        + [dma((3,))],
        compiler_params=pltpu.CompilerParams(
            collective_id=1, has_side_effects=True, vmem_limit_bytes=VMEM_LIMIT
        ),
        cost_estimate=pl.CostEstimate(flops=0, bytes_accessed=64 << 20, transcendentals=0),
    )(table, tokens, upstream, shard)


def finish_kernel(
    inverse, left_rows, root, out, rows_in, energies, chunks, spread, picked,
    a_send, a_recv, e_send, e_recv, s_send, s_recv, p_send, p_recv, local
):
    me, fs = lax.axis_index("dp"), lax.axis_index("fsdp")
    z = fs % 8
    group, side = fs // 2, z % 2
    piece = z % 4
    sources = [(2 * piece + i, 2 * (4 * q + me % 4) + 1, i, q) for i in range(2) for q in range(4)]
    my_piece, my_quarter, my_cols = me // 2, group // 4, group % 4
    places = [
        (4 * cb + my_cols, 4 * rb + my_piece, 2 * rb + cb) for rb in range(8) for cb in range(2)
    ]
    barrier = pltpu.get_barrier_semaphore()

    def tell(dp, fsdp):
        pl.semaphore_signal(barrier, inc=1, device_id=(dp, fsdp), device_id_type=MESH)

    for dp, fsdp, _, _ in sources:
        @pl.when(jnp.logical_or(dp != me, fsdp != fs))
        def _(dp=dp, fsdp=fsdp):
            tell(dp, fsdp)

    def out_rows(i, q):
        return out.at[pl.ds(pl.multiple_of(HALF * i + 16 * q, 16), 16)]

    def a_copy():
        return remote(left_rows, rows_in, a_send, a_recv, me, fs + 1 - 2 * side)

    @pl.when(side == 0)
    def _():
        pl.semaphore_wait(barrier, 1)
        a_copy().start()
        a_copy().wait_send()

    @pl.when(side == 1)
    def _():
        tell(me, fs - 1)
        for d in range(1, 8):
            tell(lax.rem(me + d, 8), fs)
        for d in range(1, NB):
            tell(me, lax.rem(fs + 2 * d, 32))
        is_own = jnp.int32(0)
        for dp, fsdp, _ in places:
            is_own += jnp.where(jnp.logical_and(dp == me, fsdp == fs), 1, 0)
        pl.semaphore_wait(barrier, 7 + 15 + 16 - is_own)

        a_copy().wait_recv()
        product = jnp.dot(
            rows_in[...], root[...], precision=lax.Precision.HIGHEST, preferred_element_type=jnp.float32
        )
        energy = jnp.sum(product * product)
        energies[0] = jnp.full((8, 128), energy, jnp.float32)

        def e_copy(d):
            return remote(
                energies.at[0], energies.at[d], e_send.at[d], e_recv.at[d], lax.rem(me + d, 8), fs
            )

        for d in range(1, 8):
            e_copy(d).start()
        for d in range(1, 8):
            e_copy(d).wait_recv()

        total = jnp.zeros((8, 128), jnp.float32)
        for dp in range(8):
            total = total + energies[lax.rem(me - dp + 8, 8)]
        mean = total[0:1, 0:1] / (BS * BS)
        update = (product / jnp.sqrt(mean + NORM_EPSILON)).astype(jnp.bfloat16)
        for j in range(NB):
            q, k = j // 4, j % 4
            chunks[j] = update[16 * q : 16 * q + 16, 128 * k : 128 * k + 128]

        def s_copy(d):
            to = lax.rem(group + d, NB)
            return remote(
                chunks.at[to], spread.at[group], s_send.at[d], s_recv.at[d], me, 2 * to + 1
            )

        for d in range(1, NB):
            s_copy(d).start()
        spread[group] = chunks[group]
        for d in range(1, NB):
            source = lax.rem(group + NB - d, NB)
            remote(
                chunks.at[0], spread.at[source], s_send.at[d], s_recv.at[d], me, 2 * source + 1
            ).wait_recv()
        for dp, fsdp, b in places:
            picked[b] = spread[inverse[b]]

        def p_copy(dp, fsdp, b):
            i, q = me % 2, my_quarter
            return remote(picked.at[b], out_rows(i, q), p_send.at[b], p_recv.at[4 * i + q], dp, fsdp)

        for dp, fsdp, b in places:
            mine = jnp.logical_and(dp == me, fsdp == fs)

            @pl.when(mine)
            def _(b=b):
                copy = pltpu.make_async_copy(picked.at[b], out_rows(me % 2, my_quarter), local)
                copy.start()
                copy.wait()

            @pl.when(jnp.logical_not(mine))
            def _(dp=dp, fsdp=fsdp, b=b):
                p_copy(dp, fsdp, b).start()

        for d in range(1, 8):
            e_copy(d).wait_send()
        for d in range(1, NB):
            s_copy(d).wait_send()
        for dp, fsdp, b in places:
            @pl.when(jnp.logical_or(dp != me, fsdp != fs))
            def _(dp=dp, fsdp=fsdp, b=b):
                p_copy(dp, fsdp, b).wait_send()

    for dp, fsdp, i, q in sources:
        @pl.when(jnp.logical_or(dp != me, fsdp != fs))
        def _(dp=dp, fsdp=fsdp, i=i, q=q):
            remote(picked.at[0], out_rows(i, q), p_send.at[0], p_recv.at[4 * i + q], dp, fsdp).wait_recv()


def finish(inverse, left_rows, root):
    dma = pltpu.SemaphoreType.DMA
    f32, b16 = jnp.float32, jnp.bfloat16
    vmem = pl.BlockSpec(memory_space=pltpu.VMEM)
    return pl.pallas_call(
        finish_kernel,
        out_shape=jax.ShapeDtypeStruct((128, 128), b16),
        in_specs=[pl.BlockSpec(memory_space=pltpu.SMEM), vmem, vmem],
        out_specs=vmem,
        scratch_shapes=[
            pltpu.VMEM((HALF, BS), f32),
            pltpu.VMEM((8, 8, 128), f32),
            pltpu.VMEM((NB, 16, 128), b16),
            pltpu.VMEM((NB, 16, 128), b16),
            pltpu.VMEM((NB, 16, 128), b16),
            dma(()),
            dma(()),
            dma((8,)),
            dma((8,)),
            dma((NB,)),
            dma((NB,)),
            dma((NB,)),
            dma((8,)),
            dma(()),
        ],
        compiler_params=pltpu.CompilerParams(
            collective_id=2, has_side_effects=True, vmem_limit_bytes=VMEM_LIMIT
        ),
        cost_estimate=pl.CostEstimate(flops=0, bytes_accessed=32 << 20, transcendentals=0),
    )(inverse, left_rows, root)


def mm(left, right):
    return jnp.dot(left, right, precision=HIGH, preferred_element_type=jnp.float32)


def newton(grad_block, stats_prev, root_prev, is_left):
    chosen = jnp.where(is_left, grad_block, grad_block.T)
    gram = mm(chosen, chosen.T)
    stats = STAT_DECAY * stats_prev + (1.0 - STAT_DECAY) * gram
    normed = stats / (jnp.trace(stats) / BS)
    identity = jnp.eye(BS, dtype=jnp.float32)
    square = mm(root_prev, root_prev)
    moment = mm(mm(square, square), normed)
    factor = (5.0 * identity - moment) * 0.25
    iterate = mm(root_prev, factor)
    factor_sq = mm(factor, factor)
    moment = mm(mm(factor_sq, factor_sq), moment)
    factor = (5.0 * identity - moment) * 0.25
    return mm(iterate, factor)


def local(tokens, upstream, weight, owner_table, stats_prev, roots_prev):
    dp, fs = lax.axis_index("dp"), lax.axis_index("fsdp")
    grad_block, full_weight = gradient_blocks(owner_table, tokens, upstream, weight)
    full_weight = full_weight.reshape(-1, weight.shape[1])
    is_left = fs % 2 == 0
    root = newton(grad_block, stats_prev[0], roots_prev[0], is_left)
    left_rows = mm(lax.dynamic_slice_in_dim(root, dp * HALF, HALF, 0), grad_block)
    positions = jnp.arange(NB, dtype=jnp.int32)
    inverse = jnp.sum(
        jnp.where(owner_table[None, :] == positions[:, None], positions[None, :], 0), axis=1
    )
    direction = finish(inverse, left_rows, root)

    tokens, upstream, direction = lax.optimization_barrier((tokens, upstream, direction))
    projected = jnp.dot(tokens, full_weight, preferred_element_type=jnp.float32).astype(jnp.bfloat16)
    input_grad = lax.dot_general(
        upstream, full_weight, (((1,), (1,)), ((), ())), preferred_element_type=jnp.float32
    ).astype(jnp.bfloat16)
    return projected, input_grad, root[None], direction


def solution(mesh):
    placed = (
        P(("dp", "fsdp"), None),
        P(("dp", "fsdp"), None),
        P("fsdp", None),
        P(),
        P("fsdp", None, None),
        P("fsdp", None, None),
    )
    return jax.shard_map(
        local,
        mesh=mesh,
        in_specs=placed,
        out_specs=(
            P(("dp", "fsdp"), None),
            P(("dp", "fsdp"), None),
            P("fsdp", None, None),
            P("fsdp", "dp"),
        ),
        check_vma=False,
    )
```

```python
import jax
import jax.numpy as jnp
from jax import lax
from jax.experimental import pallas as pl
from jax.experimental.pallas import tpu as pltpu
from jax.sharding import PartitionSpec as P

STAT_DECAY = 0.8
NORM_EPSILON = 1e-06
MESH = pl.DeviceIdType.MESH
VMEM_LIMIT = 60 * 1024 * 1024

NX, NY, NZ = 4, 4, 8
BS = 512
ROWS = 128
COLS = 256
HALF = 64
NB = 16
RA = 48
WA = 768


def remote(src, dst, send, recv, dp, fsdp):
    return pltpu.make_async_remote_copy(
        src_ref=src,
        dst_ref=dst,
        send_sem=send,
        recv_sem=recv,
        device_id=(dp, fsdp),
        device_id_type=MESH,
    )


def lanes(start, size):
    return pl.ds(pl.multiple_of(start, 128), size)


def dot3(left, right, contract=((1,), (0,))):
    def split(a):
        high = a.astype(jnp.bfloat16)
        return high, (a - high.astype(jnp.float32)).astype(jnp.bfloat16)

    def one(a, b):
        return lax.dot_general(a, b, (contract, ((), ())), preferred_element_type=jnp.float32)

    (lh, ll), (rh, rl) = split(left), split(right)
    return one(lh, rh) + (one(lh, rl) + one(ll, rh))


def update_kernel(
    table, tok, ups, shard, stats_prev, root_prev,
    projected, input_grad, root, out,
    block, weight, tok_own, ups_own, stats, start, square, fourth, moment, factor, iterate,
    projected_sum, rows_out, rows_in, energies, chunks, spread, picked,
    tok_in, tok_t, ups_in, part, outgoing, xa_in, za_sum, za_in, zb_in, xb_sum, xb_in,
    t_send, t_recv, f_send, f_recv, u_send, u_recv,
    xa_send, xa_recv, za_send, za_recv, zb_send, zb_recv, xb_send, xb_recv,
    g_send, g_recv, h_send, h_recv,
    wza_send, wza_recv, wxa_send, wxa_recv, wzb_send, wzb_recv, wxb_send, wxb_recv,
    wy_send, wy_recv, wc_send, wc_recv, own,
    a_send, a_recv, e_send, e_recv, s_send, s_recv, p_send, p_recv,
):
    me, fs = lax.axis_index("dp"), lax.axis_index("fsdp")
    y, core, x, z = me // 2, me % 2, fs // 8, fs % 8
    side = z % 2
    sibling = y * 2 + 1 - core
    mate = x * 8 + z + 1 - 2 * side

    def to_x(d):
        return lax.rem(x + d, 4)

    def to_y(d):
        return lax.rem(y + d, 4)

    def to_z(d):
        return lax.rem(z + d, 8)

    peers = [(lax.rem(me + d, 8), fs) for d in range(1, 8)]
    peers += [(me, to_x(d) * 8 + z) for d in range(1, 4)]
    peers += [(me, x * 8 + to_z(d)) for d in range(1, 8)]
    peers += [(to_y(d) * 2 + core, mate) for d in range(1, 4)]

    group, piece = fs // 2, z % 4
    sources = [(2 * piece + i, 2 * (4 * q + me % 4) + 1, i, q) for i in range(2) for q in range(4)]
    my_quarter, my_cols = group // 4, group % 4
    places = [
        (4 * b + my_cols, 4 * r + me // 2, 2 * r + b) for r in range(8) for b in range(2)
    ]

    def away(dp, fsdp):
        return jnp.logical_or(dp != me, fsdp != fs)

    barrier = pltpu.get_barrier_semaphore()

    def tell(dp, fsdp):
        pl.semaphore_signal(barrier, inc=1, device_id=(dp, fsdp), device_id_type=MESH)

    for dp, fsdp, _, _ in sources:
        @pl.when(away(dp, fsdp))
        def _(dp=dp, fsdp=fsdp):
            tell(dp, fsdp)

    @pl.when(side == 1)
    def _():
        for d in range(1, NB):
            tell(me, lax.rem(fs + 2 * d, 32))

    for dp, fsdp in peers:
        tell(dp, fsdp)

    local = [
        pltpu.make_async_copy(root_prev, start, own.at[3]),
        pltpu.make_async_copy(stats_prev, stats, own.at[4]),
        pltpu.make_async_copy(tok, tok_own, own.at[5]),
        pltpu.make_async_copy(ups, ups_own, own.at[6]),
    ]
    for copy in local:
        copy.start()

    @pl.when(side == 0)
    def _():
        pl.semaphore_wait(barrier, len(peers))

    @pl.when(side == 1)
    def _():
        at_home = jnp.int32(0)
        for dp, fsdp, _ in places:
            at_home += jnp.where(away(dp, fsdp), 0, 1)
        pl.semaphore_wait(barrier, len(peers) + NB - 1 + NB - at_home)

    def token_parts(of_y, where):
        for r in range(8):
            yield tok.at[:, lanes(512 * r + 128 * of_y, 128)], where.at[me, :, pl.ds(128 * r, 128)]

    def upstream_parts(of_core):
        for b in range(2):
            yield ups.at[:, lanes(512 * b + 256 * of_core, 256)], ups_in.at[b, me]

    for d in (2, 1, 3):
        for src, dst in token_parts(to_y(d), tok_in):
            remote(src, dst, t_send.at[d], t_recv.at[d], to_y(d) * 2 + core, fs).start()
    for src, dst in token_parts(y, tok_in):
        remote(src, dst, f_send.at[0], f_recv.at[0], sibling, fs).start()

    own_rows = pl.ds(pl.multiple_of(64 * (y % 2) + 32 * core, 32), 32)
    other_rows = pl.ds(pl.multiple_of(64 * (1 - y % 2) + 32 * core, 32), 32)
    ca, cb = pl.ds(0, WA), pl.ds(WA, 1024 - WA)

    def wza(d):
        return remote(
            shard.at[own_rows, ca], weight.at[x, z, own_rows, ca],
            wza_send.at[d], wza_recv.at[d], me, x * 8 + to_z(d),
        )

    def wxb(d):
        return remote(
            shard.at[own_rows, cb], weight.at[x, z, own_rows, cb],
            wxb_send.at[d], wxb_recv.at[d], me, to_x(d) * 8 + z,
        )

    def wxa(d):
        slab = weight.at[x, :, own_rows, ca]
        return remote(slab, slab, wxa_send.at[d], wxa_recv.at[d], me, to_x(d) * 8 + z)

    def wzb(d):
        slab = weight.at[:, z, own_rows, cb]
        return remote(slab, slab, wzb_send.at[d], wzb_recv.at[d], me, x * 8 + to_z(d))

    def wza_in(d):
        spot = weight.at[x, lax.rem(z + 8 - d, 8), own_rows, ca]
        return remote(spot, spot, wza_send.at[d], wza_recv.at[d], me, mate)

    def wxb_in(d):
        spot = weight.at[lax.rem(x + 4 - d, 4), z, own_rows, cb]
        return remote(spot, spot, wxb_send.at[d], wxb_recv.at[d], me, mate)

    def wxa_in(d):
        spot = weight.at[lax.rem(x + 4 - d, 4), :, own_rows, ca]
        return remote(spot, spot, wxa_send.at[d], wxa_recv.at[d], me, mate)

    def wzb_in(d):
        spot = weight.at[:, lax.rem(z + 8 - d, 8), own_rows, cb]
        return remote(spot, spot, wzb_send.at[d], wzb_recv.at[d], me, mate)

    own_shard = pltpu.make_async_copy(shard.at[own_rows], weight.at[x, z, own_rows], own.at[2])
    own_shard.start()
    for d in (4, 3, 5, 2, 6, 1, 7):
        wza(d).start()
    for d in (2, 1, 3):
        wxb(d).start()

    for d in (2, 1, 3, 0):
        for flip in range(2):
            if d == 0 and flip == 0:
                continue
            of_core = core if flip == 0 else 1 - core
            for src, dst in upstream_parts(of_core):
                k = 2 * d + flip
                remote(src, dst, u_send.at[k], u_recv.at[k], to_y(d) * 2 + of_core, fs).start()
    for src, dst in token_parts(y, tok_in):
        pltpu.make_async_copy(src, dst, own.at[0]).start()
    for src, dst in upstream_parts(core):
        pltpu.make_async_copy(src, dst, own.at[1]).start()

    def whole(send, recv, slot):
        return remote(tok_in.at[slot], tok_in.at[slot], send, recv, sibling, fs)

    def turn(slot):
        tok_t[:, lanes(slot * 128, 128)] = tok_in[slot].T

    pltpu.make_async_copy(tok_in.at[me], tok_in.at[me], own.at[0]).wait()
    turn(me)
    whole(f_send.at[0], f_recv.at[0], sibling).wait_recv()
    turn(sibling)

    local[0].wait()
    square[...] = dot3(start[...], start[...])

    own_shard.wait()
    for d in (1, 3, 2):
        wxb_in(d).wait_recv()
    for d in (4, 3, 5, 2, 6, 1, 7):
        wzb(d).start()
    for d in (1, 7, 2, 6, 3, 5, 4):
        wza_in(d).wait_recv()
    for d in (2, 1, 3):
        wxa(d).start()

    fourth[...] = dot3(square[...], square[...])

    for d in (1, 3, 2):
        slot = lax.rem(y + 4 - d, 4) * 2 + core
        whole(t_send.at[d], t_recv.at[d], slot).wait_recv()
        whole(f_send.at[d], f_recv.at[d], slot).start()
        turn(slot)
    for d in (1, 3, 2):
        slot = lax.rem(y + 4 - d, 4) * 2 + 1 - core
        whole(f_send.at[d], f_recv.at[d], slot).wait_recv()
        turn(slot)
    for d in (0, 1, 3, 2):
        for flip in range(2):
            if d == 0 and flip == 0:
                continue
            from_core = core if flip == 0 else 1 - core
            slot = lax.rem(y + 4 - d, 4) * 2 + from_core
            k = 2 * d + flip
            spot = ups_in.at[:, slot]
            remote(spot, spot, u_send.at[k], u_recv.at[k], sibling, fs).wait()
    pltpu.make_async_copy(ups_in.at[:, me], ups_in.at[:, me], own.at[1]).wait()

    def multiply(i, _):
        rows = tok_t[pl.ds(pl.multiple_of(i * 256, 256), 256), :]
        for b in range(2):
            piece = jnp.dot(
                rows, ups_in[b].reshape(1024, COLS), preferred_element_type=jnp.float32
            )
            part[b, 2 * i] = piece[:ROWS]
            part[b, 2 * i + 1] = piece[ROWS:]
        return 0

    lax.fori_loop(0, 4, multiply, 0)

    def arrange(of_x):
        def body(i, _):
            chosen = table[of_x * 4 + i]
            band = lax.div(chosen, 2)
            piece = jnp.where(lax.rem(chosen, 2) == 0, part[0, band], part[1, band])
            outgoing[of_x, 2 * i] = piece[:HALF]
            outgoing[of_x, 2 * i + 1] = piece[HALF:]
            return 0

        lax.fori_loop(0, 4, body, 0)

    rows_a, rows_b = pl.ds(0, RA), pl.ds(RA, HALF - RA)

    def xa(d):
        return remote(
            outgoing.at[to_x(d), :, rows_a], xa_in.at[d], xa_send.at[d], xa_recv.at[d], me, to_x(d) * 8 + z
        )

    def zb(d):
        return remote(
            outgoing.at[:, to_z(d), rows_b], zb_in.at[d], zb_send.at[d], zb_recv.at[d], me, x * 8 + to_z(d)
        )

    def za(d):
        return remote(za_sum.at[to_z(d)], za_in.at[d], za_send.at[d], za_recv.at[d], me, x * 8 + to_z(d))

    def xb(d):
        return remote(xb_sum.at[to_x(d)], xb_in.at[d], xb_send.at[d], xb_recv.at[d], me, to_x(d) * 8 + z)

    for d in (2, 1, 3, 0):
        arrange(to_x(d))
        if d:
            xa(d).start()
    for d in (4, 3, 5, 2, 6, 1, 7):
        zb(d).start()

    for d in (1, 3, 2):
        wxa_in(d).wait_recv()
    for d in (1, 7, 2, 6, 3, 5, 4):
        wzb_in(d).wait_recv()

    def wy(d):
        slab = weight.at[pl.ds(0 if d == 1 else 2, 2), :, own_rows]
        return remote(slab, slab, wy_send.at[d], wy_recv.at[d], to_y(d) * 2 + core, fs)

    def wy_in(d):
        return weight.at[pl.ds(0 if d == 1 else 2, 2), :, other_rows]

    def wc(k, spot):
        return remote(spot, spot, wc_send.at[k], wc_recv.at[k], sibling, fs)

    wy(1).start()
    wy(3).start()
    wc(0, weight.at[:, :, own_rows]).start()

    for d in (1, 7, 2, 6, 3, 5, 4):
        zb(d).wait_recv()
    for d in (2, 1, 3, 0):
        to = to_x(d)
        total = outgoing[to, z, RA:]
        for k in range(1, 8):
            total = total + zb_in[k, to]
        xb_sum[to] = total
        if d:
            xb(d).start()
    for d in (1, 3, 2):
        xa(d).wait_recv()
    for d in (4, 3, 5, 2, 6, 1, 7, 0):
        to = to_z(d)
        za_sum[to] = (outgoing[x, to, :RA] + xa_in[1, to]) + (xa_in[2, to] + xa_in[3, to])
        if d:
            za(d).start()

    def place(of_y, of_side, of_core):
        return block.at[
            pl.ds(pl.multiple_of(of_y * ROWS + of_side * HALF, HALF), HALF), lanes(of_core * COLS, COLS)
        ]

    mine = place(y, side, core)
    total = xb_sum[x]
    for d in (1, 3, 2):
        xb(d).wait_recv()
        total = total + xb_in[d]
    mine[rows_b] = total
    total = za_sum[z]
    for d in (1, 7, 2, 6, 3, 5, 4):
        za(d).wait_recv()
        total = total + za_in[d]
    mine[rows_a] = total

    def g_copy(d, flip, spot):
        k = 2 * d + flip
        return remote(spot, spot, g_send.at[k], g_recv.at[k], to_y(d) * 2 + core, mate if flip else fs)

    def h_copy(k, spot):
        return remote(spot, spot, h_send.at[k], h_recv.at[k], sibling, fs)

    order = [(d, flip) for d in (2, 1, 3, 0) for flip in range(2) if d or flip]
    for d, flip in order:
        g_copy(d, flip, mine).start()
    h_copy(0, mine).start()
    for d, flip in reversed(order):
        spot = place(lax.rem(y + 4 - d, 4), 1 - side if flip else side, core)
        g_copy(d, flip, spot).wait_recv()
        h_copy(2 * d + flip, spot).start()

    for d in (1, 3):
        remote(wy_in(d), wy_in(d), wy_send.at[d], wy_recv.at[d], sibling, fs).wait_recv()
        wc(d, wy_in(d)).start()

    for d in range(4):
        for flip in range(2):
            spot = place(lax.rem(y + 4 - d, 4), 1 - side if flip else side, 1 - core)
            h_copy(2 * d + flip, spot).wait()

    local[1].wait()

    @pl.when(side == 0)
    def _():
        moment[...] = dot3(block[...], block[...], ((1,), (1,)))

    @pl.when(side == 1)
    def _():
        moment[...] = dot3(block[...], block[...], ((0,), (0,)))

    diagonal = lax.broadcasted_iota(jnp.int32, (BS, BS), 0) == lax.broadcasted_iota(jnp.int32, (BS, BS), 1)
    fresh = STAT_DECAY * stats[...] + (1.0 - STAT_DECAY) * moment[...]
    trace = jnp.sum(jnp.where(diagonal, fresh, 0.0))
    stats[...] = fresh / (trace / BS)

    def next_factor():
        return (jnp.where(diagonal, 5.0, 0.0) - moment[...]) * 0.25

    moment[...] = dot3(fourth[...], stats[...])
    factor[...] = next_factor()
    square[...] = dot3(factor[...], factor[...])
    fourth[...] = dot3(square[...], square[...])
    iterate[...] = dot3(start[...], factor[...])
    moment[...] = dot3(fourth[...], moment[...])
    factor[...] = next_factor()
    root[...] = dot3(iterate[...], factor[...])

    sib_rows = pl.ds(pl.multiple_of(64 * (y % 2) + 32 * (1 - core), 32), 32)
    sib_other = pl.ds(pl.multiple_of(64 * (1 - y % 2) + 32 * (1 - core), 32), 32)
    wc(0, weight.at[:, :, sib_rows]).wait()
    for d in (1, 3):
        wc(d, weight.at[pl.ds(0 if d == 1 else 2, 2), :, sib_other]).wait()
    local[2].wait()
    local[3].wait()

    def products(i):
        band = weight[i].reshape(1024, 1024)
        here = jnp.dot(tok_own[:, 1024 * i : 1024 * i + 1024], band, preferred_element_type=jnp.float32)
        if i:
            here = here + projected_sum[...]
        if i < 3:
            projected_sum[...] = here
        else:
            projected[...] = here.astype(jnp.bfloat16)
        input_grad[:, 1024 * i : 1024 * i + 1024] = lax.dot_general(
            ups_own[...], band, (((1,), (1,)), ((), ())), preferred_element_type=jnp.float32
        ).astype(jnp.bfloat16)

    def a_copy():
        return remote(rows_out, rows_in, a_send, a_recv, me, mate)

    def e_copy(d):
        return remote(energies.at[0], energies.at[d], e_send.at[d], e_recv.at[d], lax.rem(me + d, 8), fs)

    def s_copy(d):
        to = lax.rem(group + d, NB)
        return remote(chunks.at[to], spread.at[group], s_send.at[d], s_recv.at[d], me, 2 * to + 1)

    def out_rows(i, q):
        return out.at[pl.ds(pl.multiple_of(HALF * i + 16 * q, 16), 16)]

    def p_copy(dp, fsdp, b):
        return remote(
            picked.at[b], out_rows(me % 2, my_quarter), p_send.at[b],
            p_recv.at[4 * (me % 2) + my_quarter], dp, fsdp,
        )

    def p_home(b):
        return pltpu.make_async_copy(picked.at[b], out_rows(me % 2, my_quarter), own.at[7])

    @pl.when(side == 0)
    def _():
        rows_out[...] = dot3(root[pl.ds(pl.multiple_of(me * HALF, HALF), HALF), :], block[...])
        a_copy().start()

    @pl.when(side == 1)
    def _():
        a_copy().wait_recv()
        iterate[:HALF] = dot3(rows_in[...], root[...])
        product = iterate[:HALF]
        energies[0] = jnp.full((8, 128), jnp.sum(product * product), jnp.float32)
        for d in range(1, 8):
            e_copy(d).start()

    products(0)

    @pl.when(side == 1)
    def _():
        for d in range(1, 8):
            e_copy(d).wait_recv()
        total = jnp.zeros((8, 128), jnp.float32)
        for dp in range(8):
            total = total + energies[lax.rem(me - dp + 8, 8)]
        mean = total[0:1, 0:1] / (BS * BS)
        update = (iterate[:HALF] / jnp.sqrt(mean + NORM_EPSILON)).astype(jnp.bfloat16)
        for j in range(NB):
            q, c = j // 4, j % 4
            chunks[j] = update[16 * q : 16 * q + 16, 128 * c : 128 * c + 128]
        for d in (8, 7, 9, 6, 10, 5, 11, 4, 12, 3, 13, 2, 14, 1, 15):
            s_copy(d).start()
        spread[group] = chunks[group]

    products(1)
    products(2)

    @pl.when(side == 1)
    def _():
        for d in range(1, NB):
            source = lax.rem(group + NB - d, NB)
            remote(
                chunks.at[0], spread.at[source], s_send.at[d], s_recv.at[d], me, 2 * source + 1
            ).wait_recv()
        for dp, fsdp, b in places:
            holder = jnp.int32(0)
            for g in range(1, NB):
                holder = jnp.maximum(holder, jnp.where(table[g] == b, g, 0))
            picked[b] = spread[holder]

            @pl.when(away(dp, fsdp))
            def _(dp=dp, fsdp=fsdp, b=b):
                p_copy(dp, fsdp, b).start()

            @pl.when(jnp.logical_not(away(dp, fsdp)))
            def _(b=b):
                p_home(b).start()

    products(3)

    for dp, fsdp, i, q in sources:
        @pl.when(away(dp, fsdp))
        def _(dp=dp, fsdp=fsdp, i=i, q=q):
            remote(picked.at[0], out_rows(i, q), p_send.at[0], p_recv.at[4 * i + q], dp, fsdp).wait_recv()

    @pl.when(side == 0)
    def _():
        a_copy().wait_send()

    @pl.when(side == 1)
    def _():
        for d in range(1, 8):
            e_copy(d).wait_send()
        for d in range(1, NB):
            s_copy(d).wait_send()
        for dp, fsdp, b in places:
            @pl.when(away(dp, fsdp))
            def _(dp=dp, fsdp=fsdp, b=b):
                p_copy(dp, fsdp, b).wait_send()

            @pl.when(jnp.logical_not(away(dp, fsdp)))
            def _(b=b):
                p_home(b).wait()

    for d in range(1, 4):
        whole(t_send.at[d], t_recv.at[d], me).wait_send()
        xa(d).wait_send()
        xb(d).wait_send()
        wxa(d).wait_send()
        wxb(d).wait_send()
    for d in range(4):
        whole(f_send.at[d], f_recv.at[d], me).wait_send()
    for d in range(1, 8):
        za(d).wait_send()
        zb(d).wait_send()
        wza(d).wait_send()
        wzb(d).wait_send()
    for d, flip in order:
        g_copy(d, flip, mine).wait_send()
    wy(1).wait_send()
    wy(3).wait_send()


def update(table, tokens, upstream, shard, stats_prev, root_prev):
    dma = pltpu.SemaphoreType.DMA
    f32, b16 = jnp.float32, jnp.bfloat16
    anywhere, vmem = pl.BlockSpec(memory_space=pl.ANY), pl.BlockSpec(memory_space=pltpu.VMEM)
    rows = tokens.shape[0]
    square = pltpu.VMEM((BS, BS), f32)
    return pl.pallas_call(
        update_kernel,
        out_shape=(
            jax.ShapeDtypeStruct((rows, 1024), b16),
            jax.ShapeDtypeStruct((rows, 4096), b16),
            jax.ShapeDtypeStruct((BS, BS), f32),
            jax.ShapeDtypeStruct((128, 128), b16),
        ),
        in_specs=[pl.BlockSpec(memory_space=pltpu.SMEM)] + [anywhere] * 5,
        out_specs=(vmem,) * 4,
        scratch_shapes=[
            square,
            pltpu.VMEM((NX, NZ, 128, 1024), b16),
            pltpu.VMEM((rows, 4096), b16),
            pltpu.VMEM((rows, 1024), b16),
        ]
        + [square] * 7
        + [
            pltpu.VMEM((rows, 1024), f32),
            pltpu.VMEM((HALF, BS), f32),
            pltpu.VMEM((HALF, BS), f32),
            pltpu.VMEM((8, 8, 128), f32),
            pltpu.VMEM((NB, 16, 128), b16),
            pltpu.VMEM((NB, 16, 128), b16),
            pltpu.VMEM((NB, 16, 128), b16),
            pltpu.VMEM((8, rows, 1024), b16),
            pltpu.VMEM((1024, 8 * rows), b16),
            pltpu.VMEM((2, 8, rows, COLS), b16),
            pltpu.VMEM((2, 8, ROWS, COLS), f32),
            pltpu.VMEM((NX, NZ, HALF, COLS), f32),
            pltpu.VMEM((NX, NZ, RA, COLS), f32),
            pltpu.VMEM((NZ, RA, COLS), f32),
            pltpu.VMEM((NZ, RA, COLS), f32),
            pltpu.VMEM((NZ, NX, HALF - RA, COLS), f32),
            pltpu.VMEM((NX, HALF - RA, COLS), f32),
            pltpu.VMEM((NX, HALF - RA, COLS), f32),
        ]
        + [dma((4,))] * 4
        + [dma((8,))] * 2
        + [dma((4,))] * 2
        + [dma((8,))] * 4
        + [dma((4,))] * 2
        + [dma((8,))] * 4
        + [dma((8,))] * 2
        + [dma((4,))] * 2
        + [dma((8,))] * 2
        + [dma((4,))] * 6
        + [dma((8,)), dma(()), dma(()), dma((8,)), dma((8,))]
        + [dma((NB,))] * 3
        + [dma((8,))],
        compiler_params=pltpu.CompilerParams(
            collective_id=0, has_side_effects=True, vmem_limit_bytes=VMEM_LIMIT
        ),
        cost_estimate=pl.CostEstimate(flops=0, bytes_accessed=64 << 20, transcendentals=0),
    )(table, tokens, upstream, shard, stats_prev, root_prev)


def settle_kernel(*refs):
    n = len(refs) // 2
    copies = [pltpu.make_async_copy(refs[i], refs[n + i], refs[-1].at[i]) for i in range(n)]
    for copy in copies:
        copy.start()
    for copy in copies:
        copy.wait()


def settle(*arrays):
    anywhere = pl.BlockSpec(memory_space=pl.ANY)
    return pl.pallas_call(
        settle_kernel,
        out_shape=tuple(jax.ShapeDtypeStruct(a.shape, a.dtype) for a in arrays),
        in_specs=[anywhere] * len(arrays),
        out_specs=(anywhere,) * len(arrays),
        scratch_shapes=[pltpu.SemaphoreType.DMA((len(arrays),))],
    )(*arrays)


def local(tokens, upstream, weight, owner_table, stats_prev, roots_prev):
    projected, input_grad, root, direction = settle(
        *update(owner_table, tokens, upstream, weight, stats_prev[0], roots_prev[0])
    )
    return projected, input_grad, root[None], direction


def solution(mesh):
    placed = (
        P(("dp", "fsdp"), None),
        P(("dp", "fsdp"), None),
        P("fsdp", None),
        P(),
        P("fsdp", None, None),
        P("fsdp", None, None),
    )
    return jax.shard_map(
        local,
        mesh=mesh,
        in_specs=placed,
        out_specs=(
            P(("dp", "fsdp"), None),
            P(("dp", "fsdp"), None),
            P("fsdp", None, None),
            P("fsdp", "dp"),
        ),
        check_vma=False,
    )
```

```python
import jax
import jax.numpy as jnp
from jax import lax
from jax.experimental import pallas as pl
from jax.experimental.pallas import tpu as pltpu
from jax.sharding import PartitionSpec as P

STAT_DECAY = 0.8
NORM_EPSILON = 1e-06
MESH = pl.DeviceIdType.MESH
VMEM_LIMIT = 60 * 1024 * 1024

NX, NY, NZ = 4, 4, 8
BS = 512
ROWS = 128
COLS = 256
HALF = 64
NB = 16
RA = 48
WA = 768


def remote(src, dst, send, recv, dp, fsdp):
    return pltpu.make_async_remote_copy(
        src_ref=src,
        dst_ref=dst,
        send_sem=send,
        recv_sem=recv,
        device_id=(dp, fsdp),
        device_id_type=MESH,
    )


def lanes(start, size):
    return pl.ds(pl.multiple_of(start, 128), size)


def dot3(left, right, contract=((1,), (0,))):
    def split(a):
        high = a.astype(jnp.bfloat16)
        return high, (a - high.astype(jnp.float32)).astype(jnp.bfloat16)

    def one(a, b):
        return lax.dot_general(a, b, (contract, ((), ())), preferred_element_type=jnp.float32)

    (lh, ll), (rh, rl) = split(left), split(right)
    return one(lh, rh) + (one(lh, rl) + one(ll, rh))


def update_kernel(
    table, tok, ups, shard, stats_prev, root_prev,
    projected, input_grad, root, out,
    block, weight, tok_own, ups_own, stats, start, square, fourth, moment, factor, iterate,
    projected_sum, rows_out, rows_in, energies, chunks, spread, picked,
    tok_in, tok_t, ups_in, part, outgoing, xa_in, za_sum, za_in, zb_in, xb_sum, xb_in,
    t_send, t_recv, f_send, f_recv, u_send, u_recv,
    xa_send, xa_recv, za_send, za_recv, zb_send, zb_recv, xb_send, xb_recv,
    g_send, g_recv, h_send, h_recv,
    wza_send, wza_recv, wxa_send, wxa_recv, wzb_send, wzb_recv, wxb_send, wxb_recv,
    wy_send, wy_recv, wc_send, wc_recv, own,
    a_send, a_recv, e_send, e_recv, s_send, s_recv, p_send, p_recv,
):
    me, fs = lax.axis_index("dp"), lax.axis_index("fsdp")
    y, core, x, z = me // 2, me % 2, fs // 8, fs % 8
    side = z % 2
    sibling = y * 2 + 1 - core
    mate = x * 8 + z + 1 - 2 * side

    def to_x(d):
        return lax.rem(x + d, 4)

    def to_y(d):
        return lax.rem(y + d, 4)

    def to_z(d):
        return lax.rem(z + d, 8)

    peers = [(lax.rem(me + d, 8), fs) for d in range(1, 8)]
    peers += [(me, to_x(d) * 8 + z) for d in range(1, 4)]
    peers += [(me, x * 8 + to_z(d)) for d in range(1, 8)]
    peers += [(to_y(d) * 2 + core, mate) for d in range(1, 4)]

    group, piece = fs // 2, z % 4
    sources = [(2 * piece + i, 2 * (4 * q + me % 4) + 1, i, q) for i in range(2) for q in range(4)]
    my_quarter, my_cols = group // 4, group % 4
    places = [
        (4 * b + my_cols, 4 * r + me // 2, 2 * r + b) for r in range(8) for b in range(2)
    ]

    def away(dp, fsdp):
        return jnp.logical_or(dp != me, fsdp != fs)

    barrier = pltpu.get_barrier_semaphore()

    def tell(dp, fsdp):
        pl.semaphore_signal(barrier, inc=1, device_id=(dp, fsdp), device_id_type=MESH)

    for dp, fsdp, _, _ in sources:
        @pl.when(away(dp, fsdp))
        def _(dp=dp, fsdp=fsdp):
            tell(dp, fsdp)

    @pl.when(side == 1)
    def _():
        for d in range(1, NB):
            tell(me, lax.rem(fs + 2 * d, 32))

    for dp, fsdp in peers:
        tell(dp, fsdp)

    local = [
        pltpu.make_async_copy(root_prev, start, own.at[3]),
        pltpu.make_async_copy(stats_prev, stats, own.at[4]),
        pltpu.make_async_copy(tok, tok_own, own.at[5]),
        pltpu.make_async_copy(ups, ups_own, own.at[6]),
    ]
    for copy in local:
        copy.start()

    @pl.when(side == 0)
    def _():
        pl.semaphore_wait(barrier, len(peers))

    @pl.when(side == 1)
    def _():
        at_home = jnp.int32(0)
        for dp, fsdp, _ in places:
            at_home += jnp.where(away(dp, fsdp), 0, 1)
        pl.semaphore_wait(barrier, len(peers) + NB - 1 + NB - at_home)

    def token_parts(of_y, where):
        for r in range(8):
            yield tok.at[:, lanes(512 * r + 128 * of_y, 128)], where.at[me, :, pl.ds(128 * r, 128)]

    def upstream_parts(of_core):
        for b in range(2):
            yield ups.at[:, lanes(512 * b + 256 * of_core, 256)], ups_in.at[b, me]

    for d in (2, 1, 3):
        for src, dst in token_parts(to_y(d), tok_in):
            remote(src, dst, t_send.at[d], t_recv.at[d], to_y(d) * 2 + core, fs).start()
    for src, dst in token_parts(y, tok_in):
        remote(src, dst, f_send.at[0], f_recv.at[0], sibling, fs).start()

    own_rows = pl.ds(pl.multiple_of(64 * (y % 2) + 32 * core, 32), 32)
    other_rows = pl.ds(pl.multiple_of(64 * (1 - y % 2) + 32 * core, 32), 32)
    ca, cb = pl.ds(0, WA), pl.ds(WA, 1024 - WA)

    def wza(d):
        return remote(
            shard.at[own_rows, ca], weight.at[x, z, own_rows, ca],
            wza_send.at[d], wza_recv.at[d], me, x * 8 + to_z(d),
        )

    def wxb(d):
        return remote(
            shard.at[own_rows, cb], weight.at[x, z, own_rows, cb],
            wxb_send.at[d], wxb_recv.at[d], me, to_x(d) * 8 + z,
        )

    def wxa(d):
        slab = weight.at[x, :, own_rows, ca]
        return remote(slab, slab, wxa_send.at[d], wxa_recv.at[d], me, to_x(d) * 8 + z)

    def wzb(d):
        slab = weight.at[:, z, own_rows, cb]
        return remote(slab, slab, wzb_send.at[d], wzb_recv.at[d], me, x * 8 + to_z(d))

    def wza_in(d):
        spot = weight.at[x, lax.rem(z + 8 - d, 8), own_rows, ca]
        return remote(spot, spot, wza_send.at[d], wza_recv.at[d], me, mate)

    def wxb_in(d):
        spot = weight.at[lax.rem(x + 4 - d, 4), z, own_rows, cb]
        return remote(spot, spot, wxb_send.at[d], wxb_recv.at[d], me, mate)

    def wxa_in(d):
        spot = weight.at[lax.rem(x + 4 - d, 4), :, own_rows, ca]
        return remote(spot, spot, wxa_send.at[d], wxa_recv.at[d], me, mate)

    def wzb_in(d):
        spot = weight.at[:, lax.rem(z + 8 - d, 8), own_rows, cb]
        return remote(spot, spot, wzb_send.at[d], wzb_recv.at[d], me, mate)

    own_shard = pltpu.make_async_copy(shard.at[own_rows], weight.at[x, z, own_rows], own.at[2])
    own_shard.start()
    for d in (4, 3, 5, 2, 6, 1, 7):
        wza(d).start()
    for d in (2, 1, 3):
        wxb(d).start()

    for d in (2, 1, 3, 0):
        for flip in range(2):
            if d == 0 and flip == 0:
                continue
            of_core = core if flip == 0 else 1 - core
            for src, dst in upstream_parts(of_core):
                k = 2 * d + flip
                remote(src, dst, u_send.at[k], u_recv.at[k], to_y(d) * 2 + of_core, fs).start()
    for src, dst in token_parts(y, tok_in):
        pltpu.make_async_copy(src, dst, own.at[0]).start()
    for src, dst in upstream_parts(core):
        pltpu.make_async_copy(src, dst, own.at[1]).start()

    def whole(send, recv, slot):
        return remote(tok_in.at[slot], tok_in.at[slot], send, recv, sibling, fs)

    def turn(slot):
        tok_t[:, lanes(slot * 128, 128)] = tok_in[slot].T

    pltpu.make_async_copy(tok_in.at[me], tok_in.at[me], own.at[0]).wait()
    turn(me)
    whole(f_send.at[0], f_recv.at[0], sibling).wait_recv()
    turn(sibling)

    local[0].wait()
    square[...] = dot3(start[...], start[...])

    own_shard.wait()
    for d in (1, 3, 2):
        wxb_in(d).wait_recv()
    for d in (4, 3, 5, 2, 6, 1, 7):
        wzb(d).start()
    for d in (1, 7, 2, 6, 3, 5, 4):
        wza_in(d).wait_recv()
    for d in (2, 1, 3):
        wxa(d).start()

    fourth[...] = dot3(square[...], square[...])

    for d in (1, 3, 2):
        slot = lax.rem(y + 4 - d, 4) * 2 + core
        whole(t_send.at[d], t_recv.at[d], slot).wait_recv()
        whole(f_send.at[d], f_recv.at[d], slot).start()
        turn(slot)
    for d in (1, 3, 2):
        slot = lax.rem(y + 4 - d, 4) * 2 + 1 - core
        whole(f_send.at[d], f_recv.at[d], slot).wait_recv()
        turn(slot)
    for d in (0, 1, 3, 2):
        for flip in range(2):
            if d == 0 and flip == 0:
                continue
            from_core = core if flip == 0 else 1 - core
            slot = lax.rem(y + 4 - d, 4) * 2 + from_core
            k = 2 * d + flip
            spot = ups_in.at[:, slot]
            remote(spot, spot, u_send.at[k], u_recv.at[k], sibling, fs).wait()
    pltpu.make_async_copy(ups_in.at[:, me], ups_in.at[:, me], own.at[1]).wait()

    def multiply(i, _):
        rows = tok_t[pl.ds(pl.multiple_of(i * 256, 256), 256), :]
        for b in range(2):
            piece = jnp.dot(
                rows, ups_in[b].reshape(1024, COLS), preferred_element_type=jnp.float32
            )
            part[b, 2 * i] = piece[:ROWS]
            part[b, 2 * i + 1] = piece[ROWS:]
        return 0

    lax.fori_loop(0, 4, multiply, 0)

    def arrange(of_x):
        def body(i, _):
            chosen = table[of_x * 4 + i]
            band = lax.div(chosen, 2)
            piece = jnp.where(lax.rem(chosen, 2) == 0, part[0, band], part[1, band])
            outgoing[of_x, 2 * i] = piece[:HALF]
            outgoing[of_x, 2 * i + 1] = piece[HALF:]
            return 0

        lax.fori_loop(0, 4, body, 0)

    rows_a, rows_b = pl.ds(0, RA), pl.ds(RA, HALF - RA)

    def xa(d):
        return remote(
            outgoing.at[to_x(d), :, rows_a], xa_in.at[d], xa_send.at[d], xa_recv.at[d], me, to_x(d) * 8 + z
        )

    def zb(d):
        return remote(
            outgoing.at[:, to_z(d), rows_b], zb_in.at[d], zb_send.at[d], zb_recv.at[d], me, x * 8 + to_z(d)
        )

    def za(d):
        return remote(za_sum.at[to_z(d)], za_in.at[d], za_send.at[d], za_recv.at[d], me, x * 8 + to_z(d))

    def xb(d):
        return remote(xb_sum.at[to_x(d)], xb_in.at[d], xb_send.at[d], xb_recv.at[d], me, to_x(d) * 8 + z)

    for d in (2, 1, 3, 0):
        arrange(to_x(d))
        if d:
            xa(d).start()
    for d in (4, 3, 5, 2, 6, 1, 7):
        zb(d).start()

    for d in (1, 3, 2):
        wxa_in(d).wait_recv()
    for d in (1, 7, 2, 6, 3, 5, 4):
        wzb_in(d).wait_recv()

    def wy(d):
        slab = weight.at[pl.ds(0 if d == 1 else 2, 2), :, own_rows]
        return remote(slab, slab, wy_send.at[d], wy_recv.at[d], to_y(d) * 2 + core, fs)

    def wy_in(d):
        return weight.at[pl.ds(0 if d == 1 else 2, 2), :, other_rows]

    def wc(k, spot):
        return remote(spot, spot, wc_send.at[k], wc_recv.at[k], sibling, fs)

    wy(1).start()
    wy(3).start()
    wc(0, weight.at[:, :, own_rows]).start()

    for d in (1, 7, 2, 6, 3, 5, 4):
        zb(d).wait_recv()
    for d in (2, 1, 3, 0):
        to = to_x(d)
        total = outgoing[to, z, RA:]
        for k in range(1, 8):
            total = total + zb_in[k, to]
        xb_sum[to] = total
        if d:
            xb(d).start()
    for d in (1, 3, 2):
        xa(d).wait_recv()
    for d in (4, 3, 5, 2, 6, 1, 7, 0):
        to = to_z(d)
        za_sum[to] = (outgoing[x, to, :RA] + xa_in[1, to]) + (xa_in[2, to] + xa_in[3, to])
        if d:
            za(d).start()

    def place(of_y, of_side, of_core):
        return block.at[
            pl.ds(pl.multiple_of(of_y * ROWS + of_side * HALF, HALF), HALF), lanes(of_core * COLS, COLS)
        ]

    mine = place(y, side, core)
    total = xb_sum[x]
    for d in (1, 3, 2):
        xb(d).wait_recv()
        total = total + xb_in[d]
    mine[rows_b] = total
    total = za_sum[z]
    for d in (1, 7, 2, 6, 3, 5, 4):
        za(d).wait_recv()
        total = total + za_in[d]
    mine[rows_a] = total

    def g_copy(d, flip, spot):
        k = 2 * d + flip
        return remote(spot, spot, g_send.at[k], g_recv.at[k], to_y(d) * 2 + core, mate if flip else fs)

    def h_copy(k, spot):
        return remote(spot, spot, h_send.at[k], h_recv.at[k], sibling, fs)

    order = [(d, flip) for d in (2, 1, 3, 0) for flip in range(2) if d or flip]
    for d, flip in order:
        g_copy(d, flip, mine).start()
    h_copy(0, mine).start()
    for d, flip in reversed(order):
        spot = place(lax.rem(y + 4 - d, 4), 1 - side if flip else side, core)
        g_copy(d, flip, spot).wait_recv()
        h_copy(2 * d + flip, spot).start()

    for d in (1, 3):
        remote(wy_in(d), wy_in(d), wy_send.at[d], wy_recv.at[d], sibling, fs).wait_recv()
        wc(d, wy_in(d)).start()

    for d in range(4):
        for flip in range(2):
            spot = place(lax.rem(y + 4 - d, 4), 1 - side if flip else side, 1 - core)
            h_copy(2 * d + flip, spot).wait()

    local[1].wait()

    @pl.when(side == 0)
    def _():
        moment[...] = dot3(block[...], block[...], ((1,), (1,)))

    @pl.when(side == 1)
    def _():
        moment[...] = dot3(block[...], block[...], ((0,), (0,)))

    diagonal = lax.broadcasted_iota(jnp.int32, (BS, BS), 0) == lax.broadcasted_iota(jnp.int32, (BS, BS), 1)
    fresh = STAT_DECAY * stats[...] + (1.0 - STAT_DECAY) * moment[...]
    trace = jnp.sum(jnp.where(diagonal, fresh, 0.0))
    stats[...] = fresh / (trace / BS)

    def next_factor():
        return (jnp.where(diagonal, 5.0, 0.0) - moment[...]) * 0.25

    moment[...] = dot3(fourth[...], stats[...])
    factor[...] = next_factor()
    square[...] = dot3(factor[...], factor[...])
    fourth[...] = dot3(square[...], square[...])
    iterate[...] = dot3(start[...], factor[...])
    moment[...] = dot3(fourth[...], moment[...])
    factor[...] = next_factor()
    root[...] = dot3(iterate[...], factor[...])

    sib_rows = pl.ds(pl.multiple_of(64 * (y % 2) + 32 * (1 - core), 32), 32)
    sib_other = pl.ds(pl.multiple_of(64 * (1 - y % 2) + 32 * (1 - core), 32), 32)
    wc(0, weight.at[:, :, sib_rows]).wait()
    for d in (1, 3):
        wc(d, weight.at[pl.ds(0 if d == 1 else 2, 2), :, sib_other]).wait()
    local[2].wait()
    local[3].wait()

    def products(i):
        band = weight[i].reshape(1024, 1024)
        here = jnp.dot(tok_own[:, 1024 * i : 1024 * i + 1024], band, preferred_element_type=jnp.float32)
        if i:
            here = here + projected_sum[...]
        if i < 3:
            projected_sum[...] = here
        else:
            projected[...] = here.astype(jnp.bfloat16)
        input_grad[:, 1024 * i : 1024 * i + 1024] = lax.dot_general(
            ups_own[...], band, (((1,), (1,)), ((), ())), preferred_element_type=jnp.float32
        ).astype(jnp.bfloat16)

    def a_copy():
        return remote(rows_out, rows_in, a_send, a_recv, me, mate)

    def e_copy(d):
        return remote(energies.at[0], energies.at[d], e_send.at[d], e_recv.at[d], lax.rem(me + d, 8), fs)

    def s_copy(d):
        to = lax.rem(group + d, NB)
        return remote(chunks.at[to], spread.at[group], s_send.at[d], s_recv.at[d], me, 2 * to + 1)

    def out_rows(i, q):
        return out.at[pl.ds(pl.multiple_of(HALF * i + 16 * q, 16), 16)]

    def p_copy(dp, fsdp, b):
        return remote(
            picked.at[b], out_rows(me % 2, my_quarter), p_send.at[b],
            p_recv.at[4 * (me % 2) + my_quarter], dp, fsdp,
        )

    def p_home(b):
        return pltpu.make_async_copy(picked.at[b], out_rows(me % 2, my_quarter), own.at[7])

    @pl.when(side == 0)
    def _():
        rows_out[...] = dot3(root[pl.ds(pl.multiple_of(me * HALF, HALF), HALF), :], block[...])
        a_copy().start()

    @pl.when(side == 1)
    def _():
        a_copy().wait_recv()
        iterate[:HALF] = dot3(rows_in[...], root[...])
        product = iterate[:HALF]
        energies[0] = jnp.full((8, 128), jnp.sum(product * product), jnp.float32)
        for d in range(1, 8):
            e_copy(d).start()

    products(0)

    @pl.when(side == 1)
    def _():
        for d in range(1, 8):
            e_copy(d).wait_recv()
        total = jnp.zeros((8, 128), jnp.float32)
        for dp in range(8):
            total = total + energies[lax.rem(me - dp + 8, 8)]
        mean = total[0:1, 0:1] / (BS * BS)
        update = (iterate[:HALF] / jnp.sqrt(mean + NORM_EPSILON)).astype(jnp.bfloat16)
        for j in range(NB):
            q, c = j // 4, j % 4
            chunks[j] = update[16 * q : 16 * q + 16, 128 * c : 128 * c + 128]
        for d in (8, 7, 9, 6, 10, 5, 11, 4, 12, 3, 13, 2, 14, 1, 15):
            s_copy(d).start()
        spread[group] = chunks[group]

    products(1)
    products(2)

    @pl.when(side == 1)
    def _():
        for d in range(1, NB):
            source = lax.rem(group + NB - d, NB)
            remote(
                chunks.at[0], spread.at[source], s_send.at[d], s_recv.at[d], me, 2 * source + 1
            ).wait_recv()
        for dp, fsdp, b in places:
            holder = jnp.int32(0)
            for g in range(1, NB):
                holder = jnp.maximum(holder, jnp.where(table[g] == b, g, 0))
            picked[b] = spread[holder]

            @pl.when(away(dp, fsdp))
            def _(dp=dp, fsdp=fsdp, b=b):
                p_copy(dp, fsdp, b).start()

            @pl.when(jnp.logical_not(away(dp, fsdp)))
            def _(b=b):
                p_home(b).start()

    products(3)

    for dp, fsdp, i, q in sources:
        @pl.when(away(dp, fsdp))
        def _(dp=dp, fsdp=fsdp, i=i, q=q):
            remote(picked.at[0], out_rows(i, q), p_send.at[0], p_recv.at[4 * i + q], dp, fsdp).wait_recv()

    @pl.when(side == 0)
    def _():
        a_copy().wait_send()

    @pl.when(side == 1)
    def _():
        for d in range(1, 8):
            e_copy(d).wait_send()
        for d in range(1, NB):
            s_copy(d).wait_send()
        for dp, fsdp, b in places:
            @pl.when(away(dp, fsdp))
            def _(dp=dp, fsdp=fsdp, b=b):
                p_copy(dp, fsdp, b).wait_send()

            @pl.when(jnp.logical_not(away(dp, fsdp)))
            def _(b=b):
                p_home(b).wait()

    for d in range(1, 4):
        whole(t_send.at[d], t_recv.at[d], me).wait_send()
        xa(d).wait_send()
        xb(d).wait_send()
        wxa(d).wait_send()
        wxb(d).wait_send()
    for d in range(4):
        whole(f_send.at[d], f_recv.at[d], me).wait_send()
    for d in range(1, 8):
        za(d).wait_send()
        zb(d).wait_send()
        wza(d).wait_send()
        wzb(d).wait_send()
    for d, flip in order:
        g_copy(d, flip, mine).wait_send()
    wy(1).wait_send()
    wy(3).wait_send()


def update(table, tokens, upstream, shard, stats_prev, root_prev):
    dma = pltpu.SemaphoreType.DMA
    f32, b16 = jnp.float32, jnp.bfloat16
    anywhere, vmem = pl.BlockSpec(memory_space=pl.ANY), pl.BlockSpec(memory_space=pltpu.VMEM)
    rows = tokens.shape[0]
    square = pltpu.VMEM((BS, BS), f32)
    return pl.pallas_call(
        update_kernel,
        out_shape=(
            jax.ShapeDtypeStruct((rows, 1024), b16),
            jax.ShapeDtypeStruct((rows, 4096), b16),
            jax.ShapeDtypeStruct((BS, BS), f32),
            jax.ShapeDtypeStruct((128, 128), b16),
        ),
        in_specs=[pl.BlockSpec(memory_space=pltpu.SMEM)] + [anywhere] * 5,
        out_specs=(vmem,) * 4,
        scratch_shapes=[
            square,
            pltpu.VMEM((NX, NZ, 128, 1024), b16),
            pltpu.VMEM((rows, 4096), b16),
            pltpu.VMEM((rows, 1024), b16),
        ]
        + [square] * 7
        + [
            pltpu.VMEM((rows, 1024), f32),
            pltpu.VMEM((HALF, BS), f32),
            pltpu.VMEM((HALF, BS), f32),
            pltpu.VMEM((8, 8, 128), f32),
            pltpu.VMEM((NB, 16, 128), b16),
            pltpu.VMEM((NB, 16, 128), b16),
            pltpu.VMEM((NB, 16, 128), b16),
            pltpu.VMEM((8, rows, 1024), b16),
            pltpu.VMEM((1024, 8 * rows), b16),
            pltpu.VMEM((2, 8, rows, COLS), b16),
            pltpu.VMEM((2, 8, ROWS, COLS), f32),
            pltpu.VMEM((NX, NZ, HALF, COLS), f32),
            pltpu.VMEM((NX, NZ, RA, COLS), f32),
            pltpu.VMEM((NZ, RA, COLS), f32),
            pltpu.VMEM((NZ, RA, COLS), f32),
            pltpu.VMEM((NZ, NX, HALF - RA, COLS), f32),
            pltpu.VMEM((NX, HALF - RA, COLS), f32),
            pltpu.VMEM((NX, HALF - RA, COLS), f32),
        ]
        + [dma((4,))] * 4
        + [dma((8,))] * 2
        + [dma((4,))] * 2
        + [dma((8,))] * 4
        + [dma((4,))] * 2
        + [dma((8,))] * 4
        + [dma((8,))] * 2
        + [dma((4,))] * 2
        + [dma((8,))] * 2
        + [dma((4,))] * 6
        + [dma((8,)), dma(()), dma(()), dma((8,)), dma((8,))]
        + [dma((NB,))] * 3
        + [dma((8,))],
        compiler_params=pltpu.CompilerParams(
            collective_id=0, has_side_effects=True, vmem_limit_bytes=VMEM_LIMIT
        ),
        cost_estimate=pl.CostEstimate(flops=0, bytes_accessed=64 << 20, transcendentals=0),
    )(table, tokens, upstream, shard, stats_prev, root_prev)


def settle_kernel(*refs):
    n = (len(refs) - 2) // 3
    given, taken, held, come, gone = refs[:n], refs[n : 2 * n], refs[2 * n : 3 * n], refs[-2], refs[-1]
    reads = [pltpu.make_async_copy(given[i], held[i], come.at[i]) for i in range(n)]
    writes = [pltpu.make_async_copy(held[i], taken[i], gone.at[i]) for i in range(n)]
    for copy in reads:
        copy.start()
    for i in range(n):
        reads[i].wait()
        writes[i].start()
    for copy in writes:
        copy.wait()


def settle(*arrays):
    anywhere = pl.BlockSpec(memory_space=pl.ANY)
    n = len(arrays)
    return pl.pallas_call(
        settle_kernel,
        out_shape=tuple(jax.ShapeDtypeStruct(a.shape, a.dtype) for a in arrays),
        in_specs=[anywhere] * n,
        out_specs=(anywhere,) * n,
        scratch_shapes=[pltpu.VMEM(a.shape, a.dtype) for a in arrays] + [pltpu.SemaphoreType.DMA((n,))] * 2,
        compiler_params=pltpu.CompilerParams(vmem_limit_bytes=VMEM_LIMIT),
    )(*arrays)


def local(tokens, upstream, weight, owner_table, stats_prev, roots_prev):
    projected, input_grad, root, direction = settle(
        *update(owner_table, tokens, upstream, weight, stats_prev[0], roots_prev[0])
    )
    return projected, input_grad, root[None], direction


def solution(mesh):
    placed = (
        P(("dp", "fsdp"), None),
        P(("dp", "fsdp"), None),
        P("fsdp", None),
        P(),
        P("fsdp", None, None),
        P("fsdp", None, None),
    )
    return jax.shard_map(
        local,
        mesh=mesh,
        in_specs=placed,
        out_specs=(
            P(("dp", "fsdp"), None),
            P(("dp", "fsdp"), None),
            P("fsdp", None, None),
            P("fsdp", "dp"),
        ),
        check_vma=False,
    )
```

```python
import jax
import jax.numpy as jnp
from jax import lax
from jax.experimental import pallas as pl
from jax.experimental.pallas import tpu as pltpu
from jax.sharding import PartitionSpec as P

STAT_DECAY = 0.8
NORM_EPSILON = 1e-06
MESH = pl.DeviceIdType.MESH
VMEM_LIMIT = 60 * 1024 * 1024

NX, NY, NZ = 4, 4, 8
BS = 512
ROWS = 128
COLS = 256
HALF = 64
NB = 16
RA = 48
WA = 768


def remote(src, dst, send, recv, dp, fsdp):
    return pltpu.make_async_remote_copy(
        src_ref=src,
        dst_ref=dst,
        send_sem=send,
        recv_sem=recv,
        device_id=(dp, fsdp),
        device_id_type=MESH,
    )


def lanes(start, size):
    return pl.ds(pl.multiple_of(start, 128), size)


def dot3(left, right, contract=((1,), (0,))):
    def split(a):
        high = a.astype(jnp.bfloat16)
        return high, (a - high.astype(jnp.float32)).astype(jnp.bfloat16)

    def one(a, b):
        return lax.dot_general(a, b, (contract, ((), ())), preferred_element_type=jnp.float32)

    (lh, ll), (rh, rl) = split(left), split(right)
    return one(lh, rh) + (one(lh, rl) + one(ll, rh))


def update_kernel(
    table, tok, ups, shard, stats_prev, root_prev,
    projected, input_grad, root, out,
    block, weight, tok_own, ups_own, stats, start, square, fourth, moment, factor, iterate,
    projected_sum, rows_out, rows_in, energies, norms, chunks, spread, picked, raw,
    tok_in, tok_t, ups_in, part, outgoing, xa_in, za_sum, za_in, zb_in, xb_sum, xb_in,
    t_send, t_recv, f_send, f_recv, u_send, u_recv,
    xa_send, xa_recv, za_send, za_recv, zb_send, zb_recv, xb_send, xb_recv,
    g_send, g_recv, h_send, h_recv,
    wza_send, wza_recv, wxa_send, wxa_recv, wzb_send, wzb_recv, wxb_send, wxb_recv,
    wy_send, wy_recv, wf_send, wf_recv, wc_send, wc_recv, own,
    a_send, a_recv, e_send, e_recv, n_send, n_recv, s_send, s_recv, p_send, p_recv,
):
    me, fs = lax.axis_index("dp"), lax.axis_index("fsdp")
    y, core, x, z = me // 2, me % 2, fs // 8, fs % 8
    side = z % 2
    sibling = y * 2 + 1 - core
    mate = x * 8 + z + 1 - 2 * side

    def to_x(d):
        return lax.rem(x + d, 4)

    def to_y(d):
        return lax.rem(y + d, 4)

    def to_z(d):
        return lax.rem(z + d, 8)

    peers = [(me, x * 8 + to_z(d)) for d in (4, 3, 5, 2, 6, 1, 7)]
    peers += [(me, to_x(d) * 8 + z) for d in (2, 1, 3)]
    peers += [(lax.rem(me + d, 8), fs) for d in range(1, 8)]

    group, piece = fs // 2, z % 4
    sources = [(2 * piece + i, 2 * (4 * q + me % 4) + 1, i, q) for i in range(2) for q in range(4)]
    my_quarter, my_cols = group // 4, group % 4
    places = [
        (4 * b + my_cols, 4 * r + me // 2, 2 * r + b) for r in range(8) for b in range(2)
    ]

    def away(dp, fsdp):
        return jnp.logical_or(dp != me, fsdp != fs)

    barrier = pltpu.get_barrier_semaphore()

    def tell(dp, fsdp):
        pl.semaphore_signal(barrier, inc=1, device_id=(dp, fsdp), device_id_type=MESH)

    for dp, fsdp in peers:
        tell(dp, fsdp)

    local = [
        pltpu.make_async_copy(root_prev, start, own.at[3]),
        pltpu.make_async_copy(stats_prev, stats, own.at[4]),
        pltpu.make_async_copy(tok, tok_own, own.at[5]),
        pltpu.make_async_copy(ups, ups_own, own.at[6]),
    ]
    for copy in local:
        copy.start()

    pl.semaphore_wait(barrier, len(peers))

    def token_parts(of_y, where):
        for r in range(8):
            yield tok.at[:, lanes(512 * r + 128 * of_y, 128)], where.at[me, :, pl.ds(128 * r, 128)]

    def upstream_parts(of_core, half):
        for b in range(2):
            yield (
                ups.at[:, lanes(512 * b + 256 * of_core + 128 * half, 128)],
                ups_in.at[half, me, :, pl.ds(128 * b, 128)],
            )

    for d in (2, 1, 3):
        for src, dst in token_parts(to_y(d), tok_in):
            remote(src, dst, t_send.at[d], t_recv.at[d], to_y(d) * 2 + core, fs).start()
    for src, dst in token_parts(y, tok_in):
        remote(src, dst, f_send.at[0], f_recv.at[0], sibling, fs).start()

    def rows_of(of_y, of_core):
        return pl.ds(pl.multiple_of(32 * of_y + 16 * of_core, 16), 16)

    own_rows = rows_of(y, core)
    ca, cb = pl.ds(0, WA), pl.ds(WA, 1024 - WA)

    def wza(d):
        return remote(
            shard.at[own_rows, ca], weight.at[x, z, own_rows, ca],
            wza_send.at[d], wza_recv.at[d], me, x * 8 + to_z(d),
        )

    def wxb(d):
        return remote(
            shard.at[own_rows, cb], weight.at[x, z, own_rows, cb],
            wxb_send.at[d], wxb_recv.at[d], me, to_x(d) * 8 + z,
        )

    def wxa(d):
        slab = weight.at[x, :, own_rows, ca]
        return remote(slab, slab, wxa_send.at[d], wxa_recv.at[d], me, to_x(d) * 8 + z)

    def wzb(d):
        slab = weight.at[:, z, own_rows, cb]
        return remote(slab, slab, wzb_send.at[d], wzb_recv.at[d], me, x * 8 + to_z(d))

    def wza_in(d):
        spot = weight.at[x, lax.rem(z + 8 - d, 8), own_rows, ca]
        return remote(spot, spot, wza_send.at[d], wza_recv.at[d], me, mate)

    def wxb_in(d):
        spot = weight.at[lax.rem(x + 4 - d, 4), z, own_rows, cb]
        return remote(spot, spot, wxb_send.at[d], wxb_recv.at[d], me, mate)

    def wxa_in(d):
        spot = weight.at[lax.rem(x + 4 - d, 4), :, own_rows, ca]
        return remote(spot, spot, wxa_send.at[d], wxa_recv.at[d], me, mate)

    def wzb_in(d):
        spot = weight.at[:, lax.rem(z + 8 - d, 8), own_rows, cb]
        return remote(spot, spot, wzb_send.at[d], wzb_recv.at[d], me, mate)

    own_shard = pltpu.make_async_copy(shard.at[own_rows], weight.at[x, z, own_rows], own.at[8])
    own_shard.start()
    for d in (4, 3, 5, 2, 6, 1, 7):
        wza(d).start()
    for d in (2, 1, 3):
        wxb(d).start()

    for half in range(2):
        for d in (2, 1, 3, 0):
            for flip in range(2):
                if d == 0 and flip == 0:
                    continue
                of_core = core if flip == 0 else 1 - core
                for src, dst in upstream_parts(of_core, half):
                    k = 2 * d + flip
                    remote(
                        src, dst, u_send.at[half, k], u_recv.at[half, k], to_y(d) * 2 + of_core, fs
                    ).start()
    for src, dst in token_parts(y, tok_in):
        pltpu.make_async_copy(src, dst, own.at[0]).start()
    for half in range(2):
        for src, dst in upstream_parts(core, half):
            pltpu.make_async_copy(src, dst, own.at[half + 1]).start()

    def whole(send, recv, slot):
        return remote(tok_in.at[slot], tok_in.at[slot], send, recv, sibling, fs)

    def turn(slot):
        tok_t[:, lanes(slot * 128, 128)] = tok_in[slot].T

    pltpu.make_async_copy(tok_in.at[me], tok_in.at[me], own.at[0]).wait()
    turn(me)
    whole(f_send.at[0], f_recv.at[0], sibling).wait_recv()
    turn(sibling)

    local[0].wait()
    square[...] = dot3(start[...], start[...])

    own_shard.wait()
    for d in (1, 3, 2):
        wxb_in(d).wait_recv()
    for d in (1, 7, 2, 6, 3, 5, 4):
        wza_in(d).wait_recv()
    for d in (2, 1, 3):
        wxa(d).start()
    for d in (4, 3, 5, 2, 6, 1, 7):
        wzb(d).start()

    fourth[...] = dot3(square[...], square[...])

    for d in (1, 3, 2):
        slot = lax.rem(y + 4 - d, 4) * 2 + core
        whole(t_send.at[d], t_recv.at[d], slot).wait_recv()
        whole(f_send.at[d], f_recv.at[d], slot).start()
        turn(slot)
    for d in (1, 3, 2):
        slot = lax.rem(y + 4 - d, 4) * 2 + 1 - core
        whole(f_send.at[d], f_recv.at[d], slot).wait_recv()
        turn(slot)
    def upstream_arrived(half):
        for d in (0, 1, 3, 2):
            for flip in range(2):
                if d == 0 and flip == 0:
                    continue
                from_core = core if flip == 0 else 1 - core
                spot = ups_in.at[half, lax.rem(y + 4 - d, 4) * 2 + from_core]
                k = 2 * d + flip
                remote(spot, spot, u_send.at[half, k], u_recv.at[half, k], sibling, fs).wait()
        pltpu.make_async_copy(ups_in.at[half, me], ups_in.at[half, me], own.at[half + 1]).wait()

    def multiply(half):
        def body(i, _):
            rows = tok_t[pl.ds(pl.multiple_of(i * 256, 256), 256), :]
            piece = jnp.dot(
                rows, ups_in[half].reshape(1024, COLS), preferred_element_type=jnp.float32
            )
            part[half, 2 * i] = piece[:ROWS]
            part[half, 2 * i + 1] = piece[ROWS:]
            return 0

        lax.fori_loop(0, 4, body, 0)

    def arrange(half, of_x):
        def body(i, _):
            chosen = table[of_x * 4 + i]
            both = part[half, lax.div(chosen, 2)]
            piece = jnp.where(lax.rem(chosen, 2) == 0, both[:, :128], both[:, 128:])
            outgoing[half, of_x, 2 * i] = piece[:HALF]
            outgoing[half, of_x, 2 * i + 1] = piece[HALF:]
            return 0

        lax.fori_loop(0, 4, body, 0)

    rows_a, rows_b = pl.ds(0, RA), pl.ds(RA, HALF - RA)

    def xa(h, d):
        return remote(
            outgoing.at[h, to_x(d), :, rows_a], xa_in.at[h, d],
            xa_send.at[h, d], xa_recv.at[h, d], me, to_x(d) * 8 + z,
        )

    def zb(h, d):
        return remote(
            outgoing.at[h, :, to_z(d), rows_b], zb_in.at[h, d],
            zb_send.at[h, d], zb_recv.at[h, d], me, x * 8 + to_z(d),
        )

    def za(h, d):
        return remote(
            za_sum.at[h, to_z(d)], za_in.at[h, d], za_send.at[h, d], za_recv.at[h, d], me, x * 8 + to_z(d)
        )

    def xb(h, d):
        return remote(
            xb_sum.at[h, to_x(d)], xb_in.at[h, d], xb_send.at[h, d], xb_recv.at[h, d], me, to_x(d) * 8 + z
        )

    def first_sums(h):
        for d in (1, 7, 2, 6, 3, 5, 4):
            zb(h, d).wait_recv()
        for d in (2, 1, 3, 0):
            to = to_x(d)
            total = outgoing[h, to, z, RA:]
            for k in range(1, 8):
                total = total + zb_in[h, k, to]
            xb_sum[h, to] = total
            if d:
                xb(h, d).start()
        for d in (1, 3, 2):
            xa(h, d).wait_recv()
        for d in (4, 3, 5, 2, 6, 1, 7, 0):
            to = to_z(d)
            za_sum[h, to] = (outgoing[h, x, to, :RA] + xa_in[h, 1, to]) + (xa_in[h, 2, to] + xa_in[h, 3, to])
            if d:
                za(h, d).start()

    for h in range(2):
        upstream_arrived(h)
        multiply(h)
        for d in (2, 1, 3, 0):
            arrange(h, to_x(d))
            if d:
                xa(h, d).start()
        for d in (4, 3, 5, 2, 6, 1, 7):
            zb(h, d).start()

    for d in (1, 3, 2):
        wxa_in(d).wait_recv()
    for d in (1, 7, 2, 6, 3, 5, 4):
        wzb_in(d).wait_recv()

    def wy(d, spot):
        return remote(spot, spot, wy_send.at[d], wy_recv.at[d], to_y(d) * 2 + core, fs)

    def wf(d, spot):
        return remote(spot, spot, wf_send.at[d], wf_recv.at[d], to_y(d) * 2 + core, fs)

    def wc(k, spot):
        return remote(spot, spot, wc_send.at[k], wc_recv.at[k], sibling, fs)

    def rows_from(d, of_core):
        return weight.at[:, :, rows_of(lax.rem(y + 4 - d, 4), of_core)]

    def half_from(d, of_y):
        return weight.at[pl.ds(0 if d == 1 else 2, 2), :, rows_of(of_y, core)]

    wy(1, rows_from(0, core)).start()
    wy(3, rows_from(0, core)).start()
    wc(0, rows_from(0, core)).start()

    first_sums(0)

    first_sums(1)

    def place(h, of_y, of_side, of_core):
        return block.at[
            pl.ds(pl.multiple_of(of_y * ROWS + of_side * HALF, HALF), HALF),
            lanes(of_core * COLS + h * 128, 128),
        ]

    def mine(h):
        return place(h, y, side, core)

    def g_copy(h, d, flip, spot):
        k = 2 * d + flip
        return remote(
            spot, spot, g_send.at[h, k], g_recv.at[h, k], to_y(d) * 2 + core, mate if flip else fs
        )

    def h_copy(h, k, spot):
        return remote(spot, spot, h_send.at[h, k], h_recv.at[h, k], sibling, fs)

    order = [(d, flip) for d in (2, 1, 3, 0) for flip in range(2) if d or flip]
    for h in range(2):
        total = xb_sum[h, x]
        for d in (1, 3, 2):
            xb(h, d).wait_recv()
            total = total + xb_in[h, d]
        mine(h)[rows_b] = total
        total = za_sum[h, z]
        for d in (1, 7, 2, 6, 3, 5, 4):
            za(h, d).wait_recv()
            total = total + za_in[h, d]
        mine(h)[rows_a] = total
        for d, flip in order:
            g_copy(h, d, flip, mine(h)).start()
        h_copy(h, 0, mine(h)).start()

    for h in range(2):
        for d, flip in reversed(order):
            spot = place(h, lax.rem(y + 4 - d, 4), 1 - side if flip else side, core)
            g_copy(h, d, flip, spot).wait_recv()
            h_copy(h, 2 * d + flip, spot).start()

    for h in range(2):
        for d in range(4):
            for flip in range(2):
                spot = place(h, lax.rem(y + 4 - d, 4), 1 - side if flip else side, 1 - core)
                h_copy(h, 2 * d + flip, spot).wait()

    for d in (1, 3):
        wy(d, rows_from(d, core)).wait_recv()
        wf(d, half_from(d, lax.rem(y + 4 - d, 4))).start()
        wc(d, rows_from(d, core)).start()

    local[1].wait()

    @pl.when(side == 0)
    def _():
        moment[...] = dot3(block[...], block[...], ((1,), (1,)))

    @pl.when(side == 1)
    def _():
        moment[...] = dot3(block[...], block[...], ((0,), (0,)))

    diagonal = lax.broadcasted_iota(jnp.int32, (BS, BS), 0) == lax.broadcasted_iota(jnp.int32, (BS, BS), 1)
    fresh = STAT_DECAY * stats[...] + (1.0 - STAT_DECAY) * moment[...]
    trace = jnp.sum(jnp.where(diagonal, fresh, 0.0))
    stats[...] = fresh / (trace / BS)

    def next_factor():
        return (jnp.where(diagonal, 5.0, 0.0) - moment[...]) * 0.25

    moment[...] = dot3(fourth[...], stats[...])
    factor[...] = next_factor()
    square[...] = dot3(factor[...], factor[...])
    fourth[...] = dot3(square[...], square[...])
    iterate[...] = dot3(start[...], factor[...])
    moment[...] = dot3(fourth[...], moment[...])
    factor[...] = next_factor()

    def a_copy():
        return remote(rows_out, rows_in, a_send, a_recv, me, mate)

    @pl.when(side == 0)
    def _():
        mine_rows = iterate[pl.ds(pl.multiple_of(me * HALF, HALF), HALF), :]
        rows_out[...] = dot3(dot3(mine_rows, factor[...]), block[...])
        a_copy().start()

    root[...] = dot3(iterate[...], factor[...])


    local[2].wait()
    local[3].wait()

    def products(i):
        band = weight[i].reshape(1024, 1024)
        here = jnp.dot(tok_own[:, 1024 * i : 1024 * i + 1024], band, preferred_element_type=jnp.float32)
        if i:
            here = here + projected_sum[...]
        if i < 3:
            projected_sum[...] = here
        else:
            projected[...] = here.astype(jnp.bfloat16)
        input_grad[:, 1024 * i : 1024 * i + 1024] = lax.dot_general(
            ups_own[...], band, (((1,), (1,)), ((), ())), preferred_element_type=jnp.float32
        ).astype(jnp.bfloat16)

    def e_copy(d):
        return remote(energies.at[0], energies.at[d], e_send.at[d], e_recv.at[d], lax.rem(me + d, 8), fs)

    def s_copy(d):
        to = lax.rem(group + d, NB)
        return remote(chunks.at[to], spread.at[group], s_send.at[d], s_recv.at[d], me, 2 * to + 1)

    def n_copy(d):
        return remote(
            norms.at[group], norms.at[group], n_send.at[d], n_recv.at[group], me, lax.rem(fs + d, 32)
        )

    def out_rows(i, q):
        return raw.at[pl.ds(pl.multiple_of(HALF * i + 16 * q, 16), 16)]

    def p_copy(dp, fsdp, b):
        return remote(
            picked.at[b], out_rows(me % 2, my_quarter), p_send.at[b],
            p_recv.at[4 * (me % 2) + my_quarter], dp, fsdp,
        )

    def holder_of(b):
        holder = jnp.int32(0)
        for g in range(1, NB):
            holder = jnp.maximum(holder, jnp.where(table[g] == b, g, 0))
        return holder

    def p_home(b):
        return pltpu.make_async_copy(picked.at[b], out_rows(me % 2, my_quarter), own.at[7])

    @pl.when(side == 1)
    def _():
        a_copy().wait_recv()
        product = dot3(rows_in[...], root[...])
        energies[0] = jnp.full((8, 128), jnp.sum(product * product), jnp.float32)
        for d in (4, 5, 2, 3, 6, 7, 1):
            e_copy(d).start()
        for j in range(NB):
            q, c = j // 4, j % 4
            chunks[j] = product[16 * q : 16 * q + 16, 128 * c : 128 * c + 128]
        for d in (8, 7, 9, 6, 10, 5, 11, 4, 12, 3, 13, 2, 14, 1, 15):
            s_copy(d).start()
        spread[group] = chunks[group]
        for d in range(1, 8):
            e_copy(d).wait_recv()
        total = jnp.zeros((8, 128), jnp.float32)
        for dp in range(8):
            total = total + energies[lax.rem(me - dp + 8, 8)]
        norms[group] = total
        for d in range(1, 32):
            n_copy(d).start()

    for d in (1, 3):
        wf(d, half_from(d, to_y(2))).wait_recv()
    wc(2, rows_from(2, core)).start()
    for d in (0, 1, 3, 2):
        wc(d, rows_from(d, 1 - core)).wait()

    products(0)
    products(1)
    products(2)

    @pl.when(side == 1)
    def _():
        for d in range(1, NB):
            source = lax.rem(group + NB - d, NB)
            remote(
                chunks.at[0], spread.at[source], s_send.at[d], s_recv.at[d], me, 2 * source + 1
            ).wait_recv()
        for dp, fsdp, b in places:
            picked[b] = spread[holder_of(b)]

            @pl.when(away(dp, fsdp))
            def _(dp=dp, fsdp=fsdp, b=b):
                p_copy(dp, fsdp, b).start()

            @pl.when(jnp.logical_not(away(dp, fsdp)))
            def _(b=b):
                p_home(b).start()

    products(3)

    for dp, fsdp, i, q in sources:
        @pl.when(away(dp, fsdp))
        def _(dp=dp, fsdp=fsdp, i=i, q=q):
            remote(picked.at[0], out_rows(i, q), p_send.at[0], p_recv.at[4 * i + q], dp, fsdp).wait_recv()

    for g in range(NB):
        @pl.when(fs != 2 * g + 1)
        def _(g=g):
            remote(norms.at[g], norms.at[g], n_send.at[1], n_recv.at[g], me, mate).wait_recv()

    @pl.when(side == 1)
    def _():
        for dp, fsdp, b in places:
            @pl.when(jnp.logical_not(away(dp, fsdp)))
            def _(b=b):
                p_home(b).wait()

    here = 2 * (fs // 4) + me // 4
    mean = norms[holder_of(here)][0:1, 0:1] / (BS * BS)
    out[...] = (raw[...] / jnp.sqrt(mean + NORM_EPSILON)).astype(jnp.bfloat16)

    @pl.when(side == 0)
    def _():
        a_copy().wait_send()

    @pl.when(side == 1)
    def _():
        for d in range(1, 8):
            e_copy(d).wait_send()
        for d in range(1, NB):
            s_copy(d).wait_send()
        for dp, fsdp, b in places:
            @pl.when(away(dp, fsdp))
            def _(dp=dp, fsdp=fsdp, b=b):
                p_copy(dp, fsdp, b).wait_send()
        for d in range(1, 32):
            n_copy(d).wait_send()

    for d in range(1, 4):
        whole(t_send.at[d], t_recv.at[d], me).wait_send()
        wxa(d).wait_send()
        wxb(d).wait_send()
    for d in range(4):
        whole(f_send.at[d], f_recv.at[d], me).wait_send()
    for d in range(1, 8):
        wza(d).wait_send()
        wzb(d).wait_send()
    for h in range(2):
        for d in range(1, 4):
            xa(h, d).wait_send()
            xb(h, d).wait_send()
        for d in range(1, 8):
            za(h, d).wait_send()
            zb(h, d).wait_send()
        for d, flip in order:
            g_copy(h, d, flip, mine(h)).wait_send()
    for d in (1, 3):
        wy(d, rows_from(0, core)).wait_send()
        wf(d, half_from(d, y)).wait_send()


def update(table, tokens, upstream, shard, stats_prev, root_prev):
    dma = pltpu.SemaphoreType.DMA
    f32, b16 = jnp.float32, jnp.bfloat16
    anywhere, vmem = pl.BlockSpec(memory_space=pl.ANY), pl.BlockSpec(memory_space=pltpu.VMEM)
    rows = tokens.shape[0]
    square = pltpu.VMEM((BS, BS), f32)
    return pl.pallas_call(
        update_kernel,
        out_shape=(
            jax.ShapeDtypeStruct((rows, 1024), b16),
            jax.ShapeDtypeStruct((rows, 4096), b16),
            jax.ShapeDtypeStruct((BS, BS), f32),
            jax.ShapeDtypeStruct((128, 128), b16),
        ),
        in_specs=[pl.BlockSpec(memory_space=pltpu.SMEM)] + [anywhere] * 5,
        out_specs=(vmem,) * 4,
        scratch_shapes=[
            square,
            pltpu.VMEM((NX, NZ, 128, 1024), b16),
            pltpu.VMEM((rows, 4096), b16),
            pltpu.VMEM((rows, 1024), b16),
        ]
        + [square] * 7
        + [
            pltpu.VMEM((rows, 1024), f32),
            pltpu.VMEM((HALF, BS), f32),
            pltpu.VMEM((HALF, BS), f32),
            pltpu.VMEM((8, 8, 128), f32),
            pltpu.VMEM((NB, 8, 128), f32),
            pltpu.VMEM((NB, 16, 128), f32),
            pltpu.VMEM((NB, 16, 128), f32),
            pltpu.VMEM((NB, 16, 128), f32),
            pltpu.VMEM((128, 128), f32),
            pltpu.VMEM((8, rows, 1024), b16),
            pltpu.VMEM((1024, 8 * rows), b16),
            pltpu.VMEM((2, 8, rows, COLS), b16),
            pltpu.VMEM((2, 8, ROWS, COLS), f32),
            pltpu.VMEM((2, NX, NZ, HALF, 128), f32),
            pltpu.VMEM((2, NX, NZ, RA, 128), f32),
            pltpu.VMEM((2, NZ, RA, 128), f32),
            pltpu.VMEM((2, NZ, RA, 128), f32),
            pltpu.VMEM((2, NZ, NX, HALF - RA, 128), f32),
            pltpu.VMEM((2, NX, HALF - RA, 128), f32),
            pltpu.VMEM((2, NX, HALF - RA, 128), f32),
        ]
        + [dma((4,))] * 4
        + [dma((2, 8))] * 2
        + [dma((2, 4))] * 2
        + [dma((2, 8))] * 4
        + [dma((2, 4))] * 2
        + [dma((2, 8))] * 4
        + [dma((8,))] * 2
        + [dma((4,))] * 2
        + [dma((8,))] * 2
        + [dma((4,))] * 8
        + [dma((9,)), dma(()), dma(()), dma((8,)), dma((8,)), dma((32,)), dma((NB,))]
        + [dma((NB,))] * 3
        + [dma((8,))],
        compiler_params=pltpu.CompilerParams(
            collective_id=0, has_side_effects=True, vmem_limit_bytes=VMEM_LIMIT
        ),
        cost_estimate=pl.CostEstimate(flops=0, bytes_accessed=64 << 20, transcendentals=0),
    )(table, tokens, upstream, shard, stats_prev, root_prev)


def settle_kernel(*refs):
    n = (len(refs) - 2) // 3
    given, taken, held, come, gone = refs[:n], refs[n : 2 * n], refs[2 * n : 3 * n], refs[-2], refs[-1]
    reads = [pltpu.make_async_copy(given[i], held[i], come.at[i]) for i in range(n)]
    writes = [pltpu.make_async_copy(held[i], taken[i], gone.at[i]) for i in range(n)]
    for copy in reads:
        copy.start()
    for i in range(n):
        reads[i].wait()
        writes[i].start()
    for copy in writes:
        copy.wait()


def settle(*arrays):
    anywhere = pl.BlockSpec(memory_space=pl.ANY)
    n = len(arrays)
    return pl.pallas_call(
        settle_kernel,
        out_shape=tuple(jax.ShapeDtypeStruct(a.shape, a.dtype) for a in arrays),
        in_specs=[anywhere] * n,
        out_specs=(anywhere,) * n,
        scratch_shapes=[pltpu.VMEM(a.shape, a.dtype) for a in arrays] + [pltpu.SemaphoreType.DMA((n,))] * 2,
        compiler_params=pltpu.CompilerParams(vmem_limit_bytes=VMEM_LIMIT),
    )(*arrays)


def local(tokens, upstream, weight, owner_table, stats_prev, roots_prev):
    projected, input_grad, root, direction = settle(
        *update(owner_table, tokens, upstream, weight, stats_prev[0], roots_prev[0])
    )
    return projected, input_grad, root[None], direction


def solution(mesh):
    placed = (
        P(("dp", "fsdp"), None),
        P(("dp", "fsdp"), None),
        P("fsdp", None),
        P(),
        P("fsdp", None, None),
        P("fsdp", None, None),
    )
    return jax.shard_map(
        local,
        mesh=mesh,
        in_specs=placed,
        out_specs=(
            P(("dp", "fsdp"), None),
            P(("dp", "fsdp"), None),
            P("fsdp", None, None),
            P("fsdp", "dp"),
        ),
        check_vma=False,
    )
```

```python
import jax
import jax.numpy as jnp
from jax import lax
from jax.experimental import pallas as pl
from jax.experimental.pallas import tpu as pltpu
from jax.sharding import PartitionSpec as P

STAT_DECAY = 0.8
NORM_EPSILON = 1e-06
MESH = pl.DeviceIdType.MESH
VMEM_LIMIT = 60 * 1024 * 1024

NX, NY, NZ = 4, 4, 8
BS = 512
ROWS = 128
COLS = 256
HALF = 64
NB = 16
RA = 48
WA = 768


def remote(src, dst, send, recv, dp, fsdp):
    return pltpu.make_async_remote_copy(
        src_ref=src,
        dst_ref=dst,
        send_sem=send,
        recv_sem=recv,
        device_id=(dp, fsdp),
        device_id_type=MESH,
    )


def lanes(start, size):
    return pl.ds(pl.multiple_of(start, 128), size)


def dot3(left, right, contract=((1,), (0,))):
    def split(a):
        high = a.astype(jnp.bfloat16)
        return high, (a - high.astype(jnp.float32)).astype(jnp.bfloat16)

    def one(a, b):
        return lax.dot_general(a, b, (contract, ((), ())), preferred_element_type=jnp.float32)

    (lh, ll), (rh, rl) = split(left), split(right)
    return one(lh, rh) + (one(lh, rl) + one(ll, rh))


def update_kernel(
    table, tok, ups, shard, stats_prev, root_prev,
    projected, input_grad, root, out,
    block, weight, tok_own, ups_own, stats, start, square, fourth, moment, factor, iterate,
    projected_sum, rows_out, rows_in, energies, norms, chunks, spread, picked, raw,
    tok_in, tok_t, ups_in, part, outgoing, xr_in, xr_sum, xa_in, za_sum, za_in, zb_in, xb_sum, xb_in,
    t_send, t_recv, f_send, f_recv, u_send, u_recv,
    xr_send, xr_recv, xd_send, xd_recv, xa_send, xa_recv, za_send, za_recv, zb_send, zb_recv, xb_send, xb_recv,
    g_send, g_recv, h_send, h_recv,
    wza_send, wza_recv, wxa_send, wxa_recv, wzb_send, wzb_recv, wxb_send, wxb_recv,
    wy_send, wy_recv, wf_send, wf_recv, wc_send, wc_recv, own,
    a_send, a_recv, e_send, e_recv, n_send, n_recv, s_send, s_recv, p_send, p_recv,
):
    me, fs = lax.axis_index("dp"), lax.axis_index("fsdp")
    y, core, x, z = me // 2, me % 2, fs // 8, fs % 8
    side = z % 2
    sibling = y * 2 + 1 - core
    mate = x * 8 + z + 1 - 2 * side

    def to_x(d):
        return lax.rem(x + d, 4)

    def to_y(d):
        return lax.rem(y + d, 4)

    def to_z(d):
        return lax.rem(z + d, 8)

    peers = [(me, x * 8 + to_z(d)) for d in (4, 3, 5, 2, 6, 1, 7)]
    peers += [(me, to_x(d) * 8 + z) for d in (2, 1, 3)]
    peers += [(lax.rem(me + d, 8), fs) for d in range(1, 8)]

    group, piece = fs // 2, z % 4
    sources = [(2 * piece + i, 2 * (4 * q + me % 4) + 1, i, q) for i in range(2) for q in range(4)]
    my_quarter, my_cols = group // 4, group % 4
    places = [
        (4 * b + my_cols, 4 * r + me // 2, 2 * r + b) for r in range(8) for b in range(2)
    ]

    def away(dp, fsdp):
        return jnp.logical_or(dp != me, fsdp != fs)

    barrier = pltpu.get_barrier_semaphore()

    def tell(dp, fsdp):
        pl.semaphore_signal(barrier, inc=1, device_id=(dp, fsdp), device_id_type=MESH)

    for dp, fsdp in peers:
        tell(dp, fsdp)

    local = [
        pltpu.make_async_copy(root_prev, start, own.at[3]),
        pltpu.make_async_copy(stats_prev, stats, own.at[4]),
        pltpu.make_async_copy(tok, tok_own, own.at[5]),
        pltpu.make_async_copy(ups, ups_own, own.at[6]),
    ]
    for copy in local:
        copy.start()

    pl.semaphore_wait(barrier, len(peers))

    def token_parts(of_y, where):
        for r in range(8):
            yield tok.at[:, lanes(512 * r + 128 * of_y, 128)], where.at[me, :, pl.ds(128 * r, 128)]

    def upstream_parts(of_core, half):
        for b in range(2):
            yield (
                ups.at[:, lanes(512 * b + 256 * of_core + 128 * half, 128)],
                ups_in.at[half, me, :, pl.ds(128 * b, 128)],
            )

    for d in (2, 1, 3):
        for src, dst in token_parts(to_y(d), tok_in):
            remote(src, dst, t_send.at[d], t_recv.at[d], to_y(d) * 2 + core, fs).start()
    for src, dst in token_parts(y, tok_in):
        remote(src, dst, f_send.at[0], f_recv.at[0], sibling, fs).start()

    def rows_of(of_y, of_core):
        return pl.ds(pl.multiple_of(32 * of_y + 16 * of_core, 16), 16)

    own_rows = rows_of(y, core)
    ca, cb = pl.ds(0, WA), pl.ds(WA, 1024 - WA)

    def wza(d):
        return remote(
            shard.at[own_rows, ca], weight.at[x, z, own_rows, ca],
            wza_send.at[d], wza_recv.at[d], me, x * 8 + to_z(d),
        )

    def wxb(d):
        return remote(
            shard.at[own_rows, cb], weight.at[x, z, own_rows, cb],
            wxb_send.at[d], wxb_recv.at[d], me, to_x(d) * 8 + z,
        )

    def wxa(d):
        slab = weight.at[x, :, own_rows, ca]
        return remote(slab, slab, wxa_send.at[d], wxa_recv.at[d], me, to_x(d) * 8 + z)

    def wzb(d):
        slab = weight.at[:, z, own_rows, cb]
        return remote(slab, slab, wzb_send.at[d], wzb_recv.at[d], me, x * 8 + to_z(d))

    def wza_in(d):
        spot = weight.at[x, lax.rem(z + 8 - d, 8), own_rows, ca]
        return remote(spot, spot, wza_send.at[d], wza_recv.at[d], me, mate)

    def wxb_in(d):
        spot = weight.at[lax.rem(x + 4 - d, 4), z, own_rows, cb]
        return remote(spot, spot, wxb_send.at[d], wxb_recv.at[d], me, mate)

    def wxa_in(d):
        spot = weight.at[lax.rem(x + 4 - d, 4), :, own_rows, ca]
        return remote(spot, spot, wxa_send.at[d], wxa_recv.at[d], me, mate)

    def wzb_in(d):
        spot = weight.at[:, lax.rem(z + 8 - d, 8), own_rows, cb]
        return remote(spot, spot, wzb_send.at[d], wzb_recv.at[d], me, mate)

    own_shard = pltpu.make_async_copy(shard.at[own_rows], weight.at[x, z, own_rows], own.at[8])
    own_shard.start()
    for d in (4, 3, 5, 2, 6, 1, 7):
        wza(d).start()
    for d in (2, 1, 3):
        wxb(d).start()

    for half in range(2):
        for d in (2, 1, 3, 0):
            for flip in range(2):
                if d == 0 and flip == 0:
                    continue
                of_core = core if flip == 0 else 1 - core
                for src, dst in upstream_parts(of_core, half):
                    k = 2 * d + flip
                    remote(
                        src, dst, u_send.at[half, k], u_recv.at[half, k], to_y(d) * 2 + of_core, fs
                    ).start()
    for src, dst in token_parts(y, tok_in):
        pltpu.make_async_copy(src, dst, own.at[0]).start()
    for half in range(2):
        for src, dst in upstream_parts(core, half):
            pltpu.make_async_copy(src, dst, own.at[half + 1]).start()

    def whole(send, recv, slot):
        return remote(tok_in.at[slot], tok_in.at[slot], send, recv, sibling, fs)

    def turn(slot):
        tok_t[:, lanes(slot * 128, 128)] = tok_in[slot].T

    pltpu.make_async_copy(tok_in.at[me], tok_in.at[me], own.at[0]).wait()
    turn(me)
    whole(f_send.at[0], f_recv.at[0], sibling).wait_recv()
    turn(sibling)

    local[0].wait()
    square[...] = dot3(start[...], start[...])

    own_shard.wait()
    for d in (1, 3, 2):
        wxb_in(d).wait_recv()
    for d in (1, 7, 2, 6, 3, 5, 4):
        wza_in(d).wait_recv()
    for d in (2, 1, 3):
        wxa(d).start()
    for d in (4, 3, 5, 2, 6, 1, 7):
        wzb(d).start()

    fourth[...] = dot3(square[...], square[...])

    for d in (1, 3, 2):
        slot = lax.rem(y + 4 - d, 4) * 2 + core
        whole(t_send.at[d], t_recv.at[d], slot).wait_recv()
        whole(f_send.at[d], f_recv.at[d], slot).start()
        turn(slot)
    for d in (1, 3, 2):
        slot = lax.rem(y + 4 - d, 4) * 2 + 1 - core
        whole(f_send.at[d], f_recv.at[d], slot).wait_recv()
        turn(slot)
    def upstream_arrived(half):
        for d in (0, 1, 3, 2):
            for flip in range(2):
                if d == 0 and flip == 0:
                    continue
                from_core = core if flip == 0 else 1 - core
                spot = ups_in.at[half, lax.rem(y + 4 - d, 4) * 2 + from_core]
                k = 2 * d + flip
                remote(spot, spot, u_send.at[half, k], u_recv.at[half, k], sibling, fs).wait()
        pltpu.make_async_copy(ups_in.at[half, me], ups_in.at[half, me], own.at[half + 1]).wait()

    def multiply(half):
        def body(i, _):
            rows = tok_t[pl.ds(pl.multiple_of(i * 256, 256), 256), :]
            piece = jnp.dot(
                rows, ups_in[half].reshape(1024, COLS), preferred_element_type=jnp.float32
            )
            part[half, 2 * i] = piece[:ROWS]
            part[half, 2 * i + 1] = piece[ROWS:]
            return 0

        lax.fori_loop(0, 4, body, 0)

    def arrange(half, of_x):
        def body(i, _):
            chosen = table[of_x * 4 + i]
            both = part[half, lax.div(chosen, 2)]
            piece = jnp.where(lax.rem(chosen, 2) == 0, both[:, :128], both[:, 128:])
            outgoing[half, of_x, 2 * i] = piece[:HALF]
            outgoing[half, of_x, 2 * i + 1] = piece[HALF:]
            return 0

        lax.fori_loop(0, 4, body, 0)

    rows_a, rows_b = pl.ds(0, RA), pl.ds(RA, HALF - RA)

    low, high = pl.ds(0, 4), pl.ds(4, 4)

    def xr(h, i):
        src = outgoing.at[h, to_x(2), (low, high)[i], rows_a]
        return remote(src, xr_in.at[h, i], xr_send.at[h, i], xr_recv.at[h, i], me, to_x((1, 3)[i]) * 8 + z)

    def xd(h, i):
        src = outgoing.at[h, to_x((1, 3)[i]), (high, low)[i], rows_a]
        dst = xa_in.at[h, i, (high, low)[i]]
        return remote(src, dst, xd_send.at[h, i], xd_recv.at[h, i], me, to_x((1, 3)[i]) * 8 + z)

    def xa(h, i):
        dst = xa_in.at[h, i, (low, high)[i]]
        return remote(xr_sum.at[h, i], dst, xa_send.at[h, i], xa_recv.at[h, i], me, to_x((1, 3)[i]) * 8 + z)

    def relay(h):
        for i in range(2):
            xr(h, i).wait_recv()
            xr_sum[h, i] = xr_in[h, i] + outgoing[h, to_x((1, 3)[i]), (low, high)[i], rows_a]
            xa(h, i).start()

    def zb(h, d):
        return remote(
            outgoing.at[h, :, to_z(d), rows_b], zb_in.at[h, d],
            zb_send.at[h, d], zb_recv.at[h, d], me, x * 8 + to_z(d),
        )

    def za(h, d):
        return remote(
            za_sum.at[h, to_z(d)], za_in.at[h, d], za_send.at[h, d], za_recv.at[h, d], me, x * 8 + to_z(d)
        )

    def xb(h, d):
        return remote(
            xb_sum.at[h, to_x(d)], xb_in.at[h, d], xb_send.at[h, d], xb_recv.at[h, d], me, to_x(d) * 8 + z
        )

    def first_sums(h):
        for d in (1, 7, 2, 6, 3, 5, 4):
            zb(h, d).wait_recv()
        for d in (2, 1, 3, 0):
            to = to_x(d)
            total = outgoing[h, to, z, RA:]
            for k in range(1, 8):
                total = total + zb_in[h, k, to]
            xb_sum[h, to] = total
            if d:
                xb(h, d).start()
        for i in range(2):
            xd(h, i).wait_recv()
            xa(h, i).wait_recv()
        for d in (4, 3, 5, 2, 6, 1, 7, 0):
            to = to_z(d)
            za_sum[h, to] = outgoing[h, x, to, :RA] + (xa_in[h, 0, to] + xa_in[h, 1, to])
            if d:
                za(h, d).start()

    def wy(d, late, of_y):
        first, count = {(1, 0): (0, 3), (1, 1): (3, 1), (3, 0): (1, 3), (3, 1): (0, 1)}[d, late]
        spot = weight.at[pl.ds(first, count), :, rows_of(of_y, core)]
        return remote(spot, spot, wy_send.at[late, d], wy_recv.at[late, d], to_y(d) * 2 + core, fs)

    def wy_from(d, late):
        return wy(d, late, lax.rem(y + 4 - d, 4))

    def late_part(d, of_core):
        first = 3 if d == 1 else 0
        return weight.at[pl.ds(first, 1), :, rows_of(lax.rem(y + 4 - d, 4), of_core)]

    def early_part(d, of_core):
        first = 0 if d == 1 else 1
        return weight.at[pl.ds(first, 3), :, rows_of(lax.rem(y + 4 - d, 4), of_core)]

    def wf(d, spot):
        return remote(spot, spot, wf_send.at[d], wf_recv.at[d], to_y(d) * 2 + core, fs)

    def wc(k, spot):
        return remote(spot, spot, wc_send.at[k], wc_recv.at[k], sibling, fs)

    def rows_from(d, of_core):
        return weight.at[:, :, rows_of(lax.rem(y + 4 - d, 4), of_core)]

    def half_from(d, of_y):
        return weight.at[pl.ds(0 if d == 1 else 2, 2), :, rows_of(of_y, core)]

    def share():
        for d in (1, 3, 2):
            wxa_in(d).wait_recv()
        for d in (1, 7, 2, 6, 3, 5, 4):
            wzb_in(d).wait_recv()

        wy(1, 0, y).start()
        wy(3, 0, y).start()
        wc(0, rows_from(0, core)).start()

    for h in range(2):
        upstream_arrived(h)
        if h:
            share()
            relay(0)
        multiply(h)
        arrange(h, to_x(2))
        for i in range(2):
            xr(h, i).start()
        arrange(h, to_x(1))
        arrange(h, to_x(3))
        for i in range(2):
            xd(h, i).start()
        arrange(h, x)
        for d in (4, 3, 5, 2, 6, 1, 7):
            zb(h, d).start()

    first_sums(0)
    relay(1)
    first_sums(1)

    def place(h, of_y, of_side, of_core):
        return block.at[
            pl.ds(pl.multiple_of(of_y * ROWS + of_side * HALF, HALF), HALF),
            lanes(of_core * COLS + h * 128, 128),
        ]

    def mine(h):
        return place(h, y, side, core)

    def g_copy(h, d, flip, spot):
        k = 2 * d + flip
        return remote(
            spot, spot, g_send.at[h, k], g_recv.at[h, k], to_y(d) * 2 + core, mate if flip else fs
        )

    def h_copy(h, k, spot):
        return remote(spot, spot, h_send.at[h, k], h_recv.at[h, k], sibling, fs)

    order = [(d, flip) for d in (2, 1, 3, 0) for flip in range(2) if d or flip]
    for h in range(2):
        total = xb_sum[h, x]
        for d in (1, 3, 2):
            xb(h, d).wait_recv()
            total = total + xb_in[h, d]
        mine(h)[rows_b] = total
        total = za_sum[h, z]
        for d in (1, 7, 2, 6, 3, 5, 4):
            za(h, d).wait_recv()
            total = total + za_in[h, d]
        mine(h)[rows_a] = total
        for d, flip in order:
            g_copy(h, d, flip, mine(h)).start()
        h_copy(h, 0, mine(h)).start()

    for h in range(2):
        for d, flip in reversed(order):
            spot = place(h, lax.rem(y + 4 - d, 4), 1 - side if flip else side, core)
            g_copy(h, d, flip, spot).wait_recv()
            h_copy(h, 2 * d + flip, spot).start()

    for h in range(2):
        for d in range(4):
            for flip in range(2):
                spot = place(h, lax.rem(y + 4 - d, 4), 1 - side if flip else side, 1 - core)
                h_copy(h, 2 * d + flip, spot).wait()

    for d in (1, 3):
        wy_from(d, 0).wait_recv()
        wf(d, half_from(d, lax.rem(y + 4 - d, 4))).start()
        wy(d, 1, y).start()
        wc(d, early_part(d, core)).start()

    local[1].wait()

    @pl.when(side == 0)
    def _():
        moment[...] = dot3(block[...], block[...], ((1,), (1,)))

    @pl.when(side == 1)
    def _():
        moment[...] = dot3(block[...], block[...], ((0,), (0,)))

    diagonal = lax.broadcasted_iota(jnp.int32, (BS, BS), 0) == lax.broadcasted_iota(jnp.int32, (BS, BS), 1)
    fresh = STAT_DECAY * stats[...] + (1.0 - STAT_DECAY) * moment[...]
    trace = jnp.sum(jnp.where(diagonal, fresh, 0.0))
    stats[...] = fresh / (trace / BS)

    def next_factor():
        return (jnp.where(diagonal, 5.0, 0.0) - moment[...]) * 0.25

    moment[...] = dot3(fourth[...], stats[...])
    factor[...] = next_factor()
    square[...] = dot3(factor[...], factor[...])
    fourth[...] = dot3(square[...], square[...])
    iterate[...] = dot3(start[...], factor[...])
    moment[...] = dot3(fourth[...], moment[...])
    factor[...] = next_factor()

    def a_copy():
        return remote(rows_out, rows_in, a_send, a_recv, me, mate)

    @pl.when(side == 0)
    def _():
        mine_rows = iterate[pl.ds(pl.multiple_of(me * HALF, HALF), HALF), :]
        rows_out[...] = dot3(dot3(mine_rows, factor[...]), block[...])
        a_copy().start()

    root[...] = dot3(iterate[...], factor[...])


    local[2].wait()
    local[3].wait()

    def products(i):
        band = weight[i].reshape(1024, 1024)
        here = jnp.dot(tok_own[:, 1024 * i : 1024 * i + 1024], band, preferred_element_type=jnp.float32)
        if i:
            here = here + projected_sum[...]
        if i < 3:
            projected_sum[...] = here
        else:
            projected[...] = here.astype(jnp.bfloat16)
        input_grad[:, 1024 * i : 1024 * i + 1024] = lax.dot_general(
            ups_own[...], band, (((1,), (1,)), ((), ())), preferred_element_type=jnp.float32
        ).astype(jnp.bfloat16)

    def e_copy(d):
        return remote(energies.at[0], energies.at[d], e_send.at[d], e_recv.at[d], lax.rem(me + d, 8), fs)

    def s_copy(d):
        to = lax.rem(group + d, NB)
        return remote(chunks.at[to], spread.at[group], s_send.at[d], s_recv.at[d], me, 2 * to + 1)

    def n_copy(d):
        return remote(
            norms.at[group], norms.at[group], n_send.at[d], n_recv.at[group], me, lax.rem(fs + d, 32)
        )

    def out_rows(i, q):
        return raw.at[pl.ds(pl.multiple_of(HALF * i + 16 * q, 16), 16)]

    def p_copy(dp, fsdp, b):
        return remote(
            picked.at[b], out_rows(me % 2, my_quarter), p_send.at[b],
            p_recv.at[4 * (me % 2) + my_quarter], dp, fsdp,
        )

    def holder_of(b):
        holder = jnp.int32(0)
        for g in range(1, NB):
            holder = jnp.maximum(holder, jnp.where(table[g] == b, g, 0))
        return holder

    def p_home(b):
        return pltpu.make_async_copy(picked.at[b], out_rows(me % 2, my_quarter), own.at[7])

    @pl.when(side == 1)
    def _():
        a_copy().wait_recv()
        product = dot3(rows_in[...], root[...])
        energies[0] = jnp.full((8, 128), jnp.sum(product * product), jnp.float32)
        for d in (4, 5, 2, 3, 6, 7, 1):
            e_copy(d).start()
        for j in range(NB):
            q, c = j // 4, j % 4
            chunks[j] = product[16 * q : 16 * q + 16, 128 * c : 128 * c + 128]
        for d in (8, 7, 9, 6, 10, 5, 11, 4, 12, 3, 13, 2, 14, 1, 15):
            s_copy(d).start()
        spread[group] = chunks[group]
        for d in range(1, 8):
            e_copy(d).wait_recv()
        total = jnp.zeros((8, 128), jnp.float32)
        for dp in range(8):
            total = total + energies[lax.rem(me - dp + 8, 8)]
        norms[group] = total
        for d in range(1, 32):
            n_copy(d).start()


    for d in (1, 3):
        wy_from(d, 1).wait_recv()
        wc(d + 3, late_part(d, core)).start()
    for d in (1, 3):
        wf(d, half_from(d, to_y(2))).wait_recv()
    wc(2, rows_from(2, core)).start()

    @pl.when(side == 1)
    def _():
        for d in range(1, NB):
            source = lax.rem(group + NB - d, NB)
            remote(
                chunks.at[0], spread.at[source], s_send.at[d], s_recv.at[d], me, 2 * source + 1
            ).wait_recv()
        for dp, fsdp, b in places:
            picked[b] = spread[holder_of(b)]

            @pl.when(away(dp, fsdp))
            def _(dp=dp, fsdp=fsdp, b=b):
                p_copy(dp, fsdp, b).start()

            @pl.when(jnp.logical_not(away(dp, fsdp)))
            def _(b=b):
                p_home(b).start()

    wc(0, rows_from(0, 1 - core)).wait()
    wc(2, rows_from(2, 1 - core)).wait()
    for d in (1, 3):
        wc(d, early_part(d, 1 - core)).wait()
        wc(d + 3, late_part(d, 1 - core)).wait()

    for i in range(4):
        products(i)

    for dp, fsdp, i, q in sources:
        @pl.when(away(dp, fsdp))
        def _(dp=dp, fsdp=fsdp, i=i, q=q):
            remote(picked.at[0], out_rows(i, q), p_send.at[0], p_recv.at[4 * i + q], dp, fsdp).wait_recv()

    for g in range(NB):
        @pl.when(fs != 2 * g + 1)
        def _(g=g):
            remote(norms.at[g], norms.at[g], n_send.at[1], n_recv.at[g], me, mate).wait_recv()

    @pl.when(side == 1)
    def _():
        for dp, fsdp, b in places:
            @pl.when(jnp.logical_not(away(dp, fsdp)))
            def _(b=b):
                p_home(b).wait()

    here = 2 * (fs // 4) + me // 4
    mean = norms[holder_of(here)][0:1, 0:1] / (BS * BS)
    out[...] = (raw[...] / jnp.sqrt(mean + NORM_EPSILON)).astype(jnp.bfloat16)

    @pl.when(side == 0)
    def _():
        a_copy().wait_send()

    @pl.when(side == 1)
    def _():
        for d in range(1, 8):
            e_copy(d).wait_send()
        for d in range(1, NB):
            s_copy(d).wait_send()
        for dp, fsdp, b in places:
            @pl.when(away(dp, fsdp))
            def _(dp=dp, fsdp=fsdp, b=b):
                p_copy(dp, fsdp, b).wait_send()
        for d in range(1, 32):
            n_copy(d).wait_send()

    for d in range(1, 4):
        whole(t_send.at[d], t_recv.at[d], me).wait_send()
        wxa(d).wait_send()
        wxb(d).wait_send()
    for d in range(4):
        whole(f_send.at[d], f_recv.at[d], me).wait_send()
    for d in range(1, 8):
        wza(d).wait_send()
        wzb(d).wait_send()
    for h in range(2):
        for i in range(2):
            xr(h, i).wait_send()
            xd(h, i).wait_send()
            xa(h, i).wait_send()
        for d in range(1, 4):
            xb(h, d).wait_send()
        for d in range(1, 8):
            za(h, d).wait_send()
            zb(h, d).wait_send()
        for d, flip in order:
            g_copy(h, d, flip, mine(h)).wait_send()
    for d in (1, 3):
        wy(d, 0, y).wait_send()
        wy(d, 1, y).wait_send()
        wf(d, half_from(d, y)).wait_send()


def update(table, tokens, upstream, shard, stats_prev, root_prev):
    dma = pltpu.SemaphoreType.DMA
    f32, b16 = jnp.float32, jnp.bfloat16
    anywhere, vmem = pl.BlockSpec(memory_space=pl.ANY), pl.BlockSpec(memory_space=pltpu.VMEM)
    rows = tokens.shape[0]
    square = pltpu.VMEM((BS, BS), f32)
    return pl.pallas_call(
        update_kernel,
        out_shape=(
            jax.ShapeDtypeStruct((rows, 1024), b16),
            jax.ShapeDtypeStruct((rows, 4096), b16),
            jax.ShapeDtypeStruct((BS, BS), f32),
            jax.ShapeDtypeStruct((128, 128), b16),
        ),
        in_specs=[pl.BlockSpec(memory_space=pltpu.SMEM)] + [anywhere] * 5,
        out_specs=(vmem,) * 4,
        scratch_shapes=[
            square,
            pltpu.VMEM((NX, NZ, 128, 1024), b16),
            pltpu.VMEM((rows, 4096), b16),
            pltpu.VMEM((rows, 1024), b16),
        ]
        + [square] * 7
        + [
            pltpu.VMEM((rows, 1024), f32),
            pltpu.VMEM((HALF, BS), f32),
            pltpu.VMEM((HALF, BS), f32),
            pltpu.VMEM((8, 8, 128), f32),
            pltpu.VMEM((NB, 8, 128), f32),
            pltpu.VMEM((NB, 16, 128), f32),
            pltpu.VMEM((NB, 16, 128), f32),
            pltpu.VMEM((NB, 16, 128), f32),
            pltpu.VMEM((128, 128), f32),
            pltpu.VMEM((8, rows, 1024), b16),
            pltpu.VMEM((1024, 8 * rows), b16),
            pltpu.VMEM((2, 8, rows, COLS), b16),
            pltpu.VMEM((2, 8, ROWS, COLS), f32),
            pltpu.VMEM((2, NX, NZ, HALF, 128), f32),
            pltpu.VMEM((2, 2, 4, RA, 128), f32),
            pltpu.VMEM((2, 2, 4, RA, 128), f32),
            pltpu.VMEM((2, 2, NZ, RA, 128), f32),
            pltpu.VMEM((2, NZ, RA, 128), f32),
            pltpu.VMEM((2, NZ, RA, 128), f32),
            pltpu.VMEM((2, NZ, NX, HALF - RA, 128), f32),
            pltpu.VMEM((2, NX, HALF - RA, 128), f32),
            pltpu.VMEM((2, NX, HALF - RA, 128), f32),
        ]
        + [dma((4,))] * 4
        + [dma((2, 8))] * 2
        + [dma((2, 2))] * 6
        + [dma((2, 8))] * 4
        + [dma((2, 4))] * 2
        + [dma((2, 8))] * 4
        + [dma((8,))] * 2
        + [dma((4,))] * 2
        + [dma((8,))] * 2
        + [dma((4,))] * 2
        + [dma((2, 4))] * 2
        + [dma((4,))] * 2
        + [dma((8,))] * 2
        + [dma((9,)), dma(()), dma(()), dma((8,)), dma((8,)), dma((32,)), dma((NB,))]
        + [dma((NB,))] * 3
        + [dma((8,))],
        compiler_params=pltpu.CompilerParams(
            collective_id=0, has_side_effects=True, vmem_limit_bytes=VMEM_LIMIT
        ),
        cost_estimate=pl.CostEstimate(flops=0, bytes_accessed=64 << 20, transcendentals=0),
    )(table, tokens, upstream, shard, stats_prev, root_prev)


def settle_kernel(*refs):
    n = (len(refs) - 2) // 3
    given, taken, held, come, gone = refs[:n], refs[n : 2 * n], refs[2 * n : 3 * n], refs[-2], refs[-1]
    reads = [pltpu.make_async_copy(given[i], held[i], come.at[i]) for i in range(n)]
    writes = [pltpu.make_async_copy(held[i], taken[i], gone.at[i]) for i in range(n)]
    for copy in reads:
        copy.start()
    for i in range(n):
        reads[i].wait()
        writes[i].start()
    for copy in writes:
        copy.wait()


def settle(*arrays):
    anywhere = pl.BlockSpec(memory_space=pl.ANY)
    n = len(arrays)
    return pl.pallas_call(
        settle_kernel,
        out_shape=tuple(jax.ShapeDtypeStruct(a.shape, a.dtype) for a in arrays),
        in_specs=[anywhere] * n,
        out_specs=(anywhere,) * n,
        scratch_shapes=[pltpu.VMEM(a.shape, a.dtype) for a in arrays] + [pltpu.SemaphoreType.DMA((n,))] * 2,
        compiler_params=pltpu.CompilerParams(vmem_limit_bytes=VMEM_LIMIT),
    )(*arrays)


def local(tokens, upstream, weight, owner_table, stats_prev, roots_prev):
    projected, input_grad, root, direction = settle(
        *update(owner_table, tokens, upstream, weight, stats_prev[0], roots_prev[0])
    )
    return projected, input_grad, root[None], direction


def solution(mesh):
    placed = (
        P(("dp", "fsdp"), None),
        P(("dp", "fsdp"), None),
        P("fsdp", None),
        P(),
        P("fsdp", None, None),
        P("fsdp", None, None),
    )
    return jax.shard_map(
        local,
        mesh=mesh,
        in_specs=placed,
        out_specs=(
            P(("dp", "fsdp"), None),
            P(("dp", "fsdp"), None),
            P("fsdp", None, None),
            P("fsdp", "dp"),
        ),
        check_vma=False,
    )
```

```python
import jax
import jax.numpy as jnp
from jax import lax
from jax.experimental import pallas as pl
from jax.experimental.pallas import tpu as pltpu
from jax.sharding import PartitionSpec as P

STAT_DECAY = 0.8
NORM_EPSILON = 1e-06
MESH = pl.DeviceIdType.MESH
VMEM_LIMIT = 48 * 1024 * 1024

NX, NY, NZ = 4, 4, 8
BS = 512
ROWS = 128
COLS = 256
HALF = 64
NB = 16
RA = 48
WA = 768


def remote(src, dst, send, recv, dp, fsdp):
    return pltpu.make_async_remote_copy(
        src_ref=src,
        dst_ref=dst,
        send_sem=send,
        recv_sem=recv,
        device_id=(dp, fsdp),
        device_id_type=MESH,
    )


def lanes(start, size):
    return pl.ds(pl.multiple_of(start, 128), size)


def dot3(left, right, contract=((1,), (0,))):
    def split(a):
        high = a.astype(jnp.bfloat16)
        return high, (a - high.astype(jnp.float32)).astype(jnp.bfloat16)

    def one(a, b):
        return lax.dot_general(a, b, (contract, ((), ())), preferred_element_type=jnp.float32)

    (lh, ll), (rh, rl) = split(left), split(right)
    return one(lh, rh) + (one(lh, rl) + one(ll, rh))


def update_kernel(
    table, tok, ups, shard, stats_prev, root_prev,
    projected, input_grad, root, out,
    block, weight, tok_own, ups_own, stats, start, square, fourth, moment, factor, iterate,
    projected_sum, rows_out, rows_in, energies, norms, chunks, spread, picked, raw,
    tok_in, tok_t, ups_in, part, outgoing, xr_in, xr_sum, xa_in, za_sum, za_in, zb_in, xb_sum, xb_in,
    t_send, t_recv, f_send, f_recv, u_send, u_recv,
    xr_send, xr_recv, xd_send, xd_recv, xa_send, xa_recv, za_send, za_recv, zb_send, zb_recv, xb_send, xb_recv,
    g_send, g_recv, h_send, h_recv,
    wza_send, wza_recv, wxa_send, wxa_recv, wzb_send, wzb_recv, wxb_send, wxb_recv,
    wy_send, wy_recv, wf_send, wf_recv, wc_send, wc_recv, own,
    a_send, a_recv, e_send, e_recv, n_send, n_recv, s_send, s_recv, p_send, p_recv,
):
    me, fs = lax.axis_index("dp"), lax.axis_index("fsdp")
    y, core, x, z = me // 2, me % 2, fs // 8, fs % 8
    side = z % 2
    sibling = y * 2 + 1 - core
    mate = x * 8 + z + 1 - 2 * side

    def to_x(d):
        return lax.rem(x + d, 4)

    def to_y(d):
        return lax.rem(y + d, 4)

    def to_z(d):
        return lax.rem(z + d, 8)

    peers = [(me, x * 8 + to_z(d)) for d in (4, 3, 5, 2, 6, 1, 7)]
    peers += [(me, to_x(d) * 8 + z) for d in (2, 1, 3)]
    peers += [(lax.rem(me + d, 8), fs) for d in range(1, 8)]

    group, piece = fs // 2, z % 4
    sources = [(2 * piece + i, 2 * (4 * q + me % 4) + 1, i, q) for i in range(2) for q in range(4)]
    my_quarter, my_cols = group // 4, group % 4
    places = [
        (4 * b + my_cols, 4 * r + me // 2, 2 * r + b) for r in range(8) for b in range(2)
    ]

    def away(dp, fsdp):
        return jnp.logical_or(dp != me, fsdp != fs)

    barrier = pltpu.get_barrier_semaphore()

    def tell(dp, fsdp):
        pl.semaphore_signal(barrier, inc=1, device_id=(dp, fsdp), device_id_type=MESH)

    for dp, fsdp in peers:
        tell(dp, fsdp)

    local = [
        pltpu.make_async_copy(root_prev, start, own.at[3]),
        pltpu.make_async_copy(stats_prev, stats, own.at[4]),
        pltpu.make_async_copy(tok, tok_own, own.at[5]),
        pltpu.make_async_copy(ups, ups_own, own.at[6]),
    ]
    for copy in local:
        copy.start()

    pl.semaphore_wait(barrier, len(peers))

    def token_parts(of_y, where):
        for r in range(8):
            yield tok.at[:, lanes(512 * r + 128 * of_y, 128)], where.at[me, :, pl.ds(128 * r, 128)]

    def upstream_parts(of_core, half):
        for b in range(2):
            yield (
                ups.at[:, lanes(512 * b + 256 * of_core + 128 * half, 128)],
                ups_in.at[half, me, :, pl.ds(128 * b, 128)],
            )

    for d in (2, 1, 3):
        for src, dst in token_parts(to_y(d), tok_in):
            remote(src, dst, t_send.at[d], t_recv.at[d], to_y(d) * 2 + core, fs).start()
    for src, dst in token_parts(y, tok_in):
        remote(src, dst, f_send.at[0], f_recv.at[0], sibling, fs).start()

    def rows_of(of_y, of_core):
        return pl.ds(pl.multiple_of(32 * of_y + 16 * of_core, 16), 16)

    own_rows = rows_of(y, core)
    ca, cb = pl.ds(0, WA), pl.ds(WA, 1024 - WA)

    def wza(d):
        return remote(
            shard.at[own_rows, ca], weight.at[x, z, own_rows, ca],
            wza_send.at[d], wza_recv.at[d], me, x * 8 + to_z(d),
        )

    def wxb(d):
        return remote(
            shard.at[own_rows, cb], weight.at[x, z, own_rows, cb],
            wxb_send.at[d], wxb_recv.at[d], me, to_x(d) * 8 + z,
        )

    def wxa(d):
        slab = weight.at[x, :, own_rows, ca]
        return remote(slab, slab, wxa_send.at[d], wxa_recv.at[d], me, to_x(d) * 8 + z)

    def wzb(d):
        slab = weight.at[:, z, own_rows, cb]
        return remote(slab, slab, wzb_send.at[d], wzb_recv.at[d], me, x * 8 + to_z(d))

    def wza_in(d):
        spot = weight.at[x, lax.rem(z + 8 - d, 8), own_rows, ca]
        return remote(spot, spot, wza_send.at[d], wza_recv.at[d], me, mate)

    def wxb_in(d):
        spot = weight.at[lax.rem(x + 4 - d, 4), z, own_rows, cb]
        return remote(spot, spot, wxb_send.at[d], wxb_recv.at[d], me, mate)

    def wxa_in(d):
        spot = weight.at[lax.rem(x + 4 - d, 4), :, own_rows, ca]
        return remote(spot, spot, wxa_send.at[d], wxa_recv.at[d], me, mate)

    def wzb_in(d):
        spot = weight.at[:, lax.rem(z + 8 - d, 8), own_rows, cb]
        return remote(spot, spot, wzb_send.at[d], wzb_recv.at[d], me, mate)

    own_shard = pltpu.make_async_copy(shard.at[own_rows], weight.at[x, z, own_rows], own.at[8])
    own_shard.start()
    for d in (4, 3, 5, 2, 6, 1, 7):
        wza(d).start()
    for d in (2, 1, 3):
        wxb(d).start()

    for half in range(2):
        for d in (2, 1, 3, 0):
            for flip in range(2):
                if d == 0 and flip == 0:
                    continue
                of_core = core if flip == 0 else 1 - core
                for src, dst in upstream_parts(of_core, half):
                    k = 2 * d + flip
                    remote(
                        src, dst, u_send.at[half, k], u_recv.at[half, k], to_y(d) * 2 + of_core, fs
                    ).start()
    for src, dst in token_parts(y, tok_in):
        pltpu.make_async_copy(src, dst, own.at[0]).start()
    for half in range(2):
        for src, dst in upstream_parts(core, half):
            pltpu.make_async_copy(src, dst, own.at[half + 1]).start()

    def whole(send, recv, slot):
        return remote(tok_in.at[slot], tok_in.at[slot], send, recv, sibling, fs)

    def turn(slot):
        tok_t[:, lanes(slot * 128, 128)] = tok_in[slot].T

    pltpu.make_async_copy(tok_in.at[me], tok_in.at[me], own.at[0]).wait()
    turn(me)
    whole(f_send.at[0], f_recv.at[0], sibling).wait_recv()
    turn(sibling)

    local[0].wait()
    square[...] = dot3(start[...], start[...])

    own_shard.wait()
    for d in (1, 3, 2):
        wxb_in(d).wait_recv()
    for d in (1, 7, 2, 6, 3, 5, 4):
        wza_in(d).wait_recv()
    for d in (2, 1, 3):
        wxa(d).start()
    for d in (4, 3, 5, 2, 6, 1, 7):
        wzb(d).start()

    fourth[...] = dot3(square[...], square[...])

    for d in (1, 3, 2):
        slot = lax.rem(y + 4 - d, 4) * 2 + core
        whole(t_send.at[d], t_recv.at[d], slot).wait_recv()
        whole(f_send.at[d], f_recv.at[d], slot).start()
        turn(slot)
    for d in (1, 3, 2):
        slot = lax.rem(y + 4 - d, 4) * 2 + 1 - core
        whole(f_send.at[d], f_recv.at[d], slot).wait_recv()
        turn(slot)
    def upstream_arrived(half):
        for d in (0, 1, 3, 2):
            for flip in range(2):
                if d == 0 and flip == 0:
                    continue
                from_core = core if flip == 0 else 1 - core
                spot = ups_in.at[half, lax.rem(y + 4 - d, 4) * 2 + from_core]
                k = 2 * d + flip
                remote(spot, spot, u_send.at[half, k], u_recv.at[half, k], sibling, fs).wait()
        pltpu.make_async_copy(ups_in.at[half, me], ups_in.at[half, me], own.at[half + 1]).wait()

    def multiply(half):
        def body(i, _):
            rows = tok_t[pl.ds(pl.multiple_of(i * 256, 256), 256), :]
            piece = jnp.dot(
                rows, ups_in[half].reshape(1024, COLS), preferred_element_type=jnp.float32
            )
            part[half, 2 * i] = piece[:ROWS]
            part[half, 2 * i + 1] = piece[ROWS:]
            return 0

        lax.fori_loop(0, 4, body, 0)

    def arrange(half, of_x):
        def body(i, _):
            chosen = table[of_x * 4 + i]
            both = part[half, lax.div(chosen, 2)]
            piece = jnp.where(lax.rem(chosen, 2) == 0, both[:, :128], both[:, 128:])
            outgoing[half, of_x, 2 * i] = piece[:HALF]
            outgoing[half, of_x, 2 * i + 1] = piece[HALF:]
            return 0

        lax.fori_loop(0, 4, body, 0)

    rows_a, rows_b = pl.ds(0, RA), pl.ds(RA, HALF - RA)

    low, high = pl.ds(0, 4), pl.ds(4, 4)

    def xr(h, i):
        src = outgoing.at[h, to_x(2), (low, high)[i], rows_a]
        return remote(src, xr_in.at[h, i], xr_send.at[h, i], xr_recv.at[h, i], me, to_x((1, 3)[i]) * 8 + z)

    def xd(h, i):
        src = outgoing.at[h, to_x((1, 3)[i]), (high, low)[i], rows_a]
        dst = xa_in.at[h, i, (high, low)[i]]
        return remote(src, dst, xd_send.at[h, i], xd_recv.at[h, i], me, to_x((1, 3)[i]) * 8 + z)

    def xa(h, i):
        dst = xa_in.at[h, i, (low, high)[i]]
        return remote(xr_sum.at[h, i], dst, xa_send.at[h, i], xa_recv.at[h, i], me, to_x((1, 3)[i]) * 8 + z)

    def relay(h):
        for i in range(2):
            xr(h, i).wait_recv()
            xr_sum[h, i] = xr_in[h, i] + outgoing[h, to_x((1, 3)[i]), (low, high)[i], rows_a]
            xa(h, i).start()

    def zb(h, d):
        return remote(
            outgoing.at[h, :, to_z(d), rows_b], zb_in.at[h, d],
            zb_send.at[h, d], zb_recv.at[h, d], me, x * 8 + to_z(d),
        )

    def za(h, d):
        return remote(
            za_sum.at[h, to_z(d)], za_in.at[h, d], za_send.at[h, d], za_recv.at[h, d], me, x * 8 + to_z(d)
        )

    def xb(h, d):
        return remote(
            xb_sum.at[h, to_x(d)], xb_in.at[h, d], xb_send.at[h, d], xb_recv.at[h, d], me, to_x(d) * 8 + z
        )

    def first_sums(h):
        for d in (1, 7, 2, 6, 3, 5, 4):
            zb(h, d).wait_recv()
        for d in (2, 1, 3, 0):
            to = to_x(d)
            total = outgoing[h, to, z, RA:]
            for k in range(1, 8):
                total = total + zb_in[h, k, to]
            xb_sum[h, to] = total
            if d:
                xb(h, d).start()
        for i in range(2):
            xd(h, i).wait_recv()
            xa(h, i).wait_recv()
        for d in (4, 3, 5, 2, 6, 1, 7, 0):
            to = to_z(d)
            za_sum[h, to] = outgoing[h, x, to, :RA] + (xa_in[h, 0, to] + xa_in[h, 1, to])
            if d:
                za(h, d).start()

    def wy(d, late, of_y):
        first, count = {(1, 0): (0, 3), (1, 1): (3, 1), (3, 0): (1, 3), (3, 1): (0, 1)}[d, late]
        spot = weight.at[pl.ds(first, count), :, rows_of(of_y, core)]
        return remote(spot, spot, wy_send.at[late, d], wy_recv.at[late, d], to_y(d) * 2 + core, fs)

    def wy_from(d, late):
        return wy(d, late, lax.rem(y + 4 - d, 4))

    def late_part(d, of_core):
        first = 3 if d == 1 else 0
        return weight.at[pl.ds(first, 1), :, rows_of(lax.rem(y + 4 - d, 4), of_core)]

    def early_part(d, of_core):
        first = 0 if d == 1 else 1
        return weight.at[pl.ds(first, 3), :, rows_of(lax.rem(y + 4 - d, 4), of_core)]

    def wf(d, spot):
        return remote(spot, spot, wf_send.at[d], wf_recv.at[d], to_y(d) * 2 + core, fs)

    def wc(k, spot):
        return remote(spot, spot, wc_send.at[k], wc_recv.at[k], sibling, fs)

    def rows_from(d, of_core):
        return weight.at[:, :, rows_of(lax.rem(y + 4 - d, 4), of_core)]

    def half_from(d, of_y):
        return weight.at[pl.ds(0 if d == 1 else 2, 2), :, rows_of(of_y, core)]

    def share():
        for d in (1, 3, 2):
            wxa_in(d).wait_recv()
        for d in (1, 7, 2, 6, 3, 5, 4):
            wzb_in(d).wait_recv()

        wy(1, 0, y).start()
        wy(3, 0, y).start()
        wc(0, rows_from(0, core)).start()

    for h in range(2):
        upstream_arrived(h)
        if h:
            share()
            relay(0)
        multiply(h)
        arrange(h, to_x(2))
        for i in range(2):
            xr(h, i).start()
        arrange(h, to_x(1))
        arrange(h, to_x(3))
        for i in range(2):
            xd(h, i).start()
        arrange(h, x)
        for d in (4, 3, 5, 2, 6, 1, 7):
            zb(h, d).start()

    first_sums(0)
    relay(1)
    first_sums(1)

    def place(h, of_y, of_side, of_core):
        return block.at[
            pl.ds(pl.multiple_of(of_y * ROWS + of_side * HALF, HALF), HALF),
            lanes(of_core * COLS + h * 128, 128),
        ]

    def mine(h):
        return place(h, y, side, core)

    def g_copy(h, d, flip, spot):
        k = 2 * d + flip
        return remote(
            spot, spot, g_send.at[h, k], g_recv.at[h, k], to_y(d) * 2 + core, mate if flip else fs
        )

    def h_copy(h, k, spot):
        return remote(spot, spot, h_send.at[h, k], h_recv.at[h, k], sibling, fs)

    order = [(d, flip) for d in (2, 1, 3, 0) for flip in range(2) if d or flip]
    for h in range(2):
        total = xb_sum[h, x]
        for d in (1, 3, 2):
            xb(h, d).wait_recv()
            total = total + xb_in[h, d]
        mine(h)[rows_b] = total
        total = za_sum[h, z]
        for d in (1, 7, 2, 6, 3, 5, 4):
            za(h, d).wait_recv()
            total = total + za_in[h, d]
        mine(h)[rows_a] = total
        for d, flip in order:
            g_copy(h, d, flip, mine(h)).start()
        h_copy(h, 0, mine(h)).start()

    for h in range(2):
        for d, flip in reversed(order):
            spot = place(h, lax.rem(y + 4 - d, 4), 1 - side if flip else side, core)
            g_copy(h, d, flip, spot).wait_recv()
            h_copy(h, 2 * d + flip, spot).start()

    for h in range(2):
        for d in range(4):
            for flip in range(2):
                spot = place(h, lax.rem(y + 4 - d, 4), 1 - side if flip else side, 1 - core)
                h_copy(h, 2 * d + flip, spot).wait()

    for d in (1, 3):
        wy_from(d, 0).wait_recv()
        wf(d, half_from(d, lax.rem(y + 4 - d, 4))).start()
        wc(d, early_part(d, core)).start()

    local[1].wait()

    @pl.when(side == 0)
    def _():
        moment[...] = dot3(block[...], block[...], ((1,), (1,)))

    @pl.when(side == 1)
    def _():
        moment[...] = dot3(block[...], block[...], ((0,), (0,)))

    diagonal = lax.broadcasted_iota(jnp.int32, (BS, BS), 0) == lax.broadcasted_iota(jnp.int32, (BS, BS), 1)
    fresh = STAT_DECAY * stats[...] + (1.0 - STAT_DECAY) * moment[...]
    trace = jnp.sum(jnp.where(diagonal, fresh, 0.0))
    stats[...] = fresh / (trace / BS)

    def next_factor():
        return (jnp.where(diagonal, 5.0, 0.0) - moment[...]) * 0.25

    moment[...] = dot3(fourth[...], stats[...])
    factor[...] = next_factor()
    square[...] = dot3(factor[...], factor[...])
    fourth[...] = dot3(square[...], square[...])
    iterate[...] = dot3(start[...], factor[...])
    moment[...] = dot3(fourth[...], moment[...])
    factor[...] = next_factor()

    def a_copy():
        return remote(rows_out, rows_in, a_send, a_recv, me, mate)

    @pl.when(side == 0)
    def _():
        mine_rows = iterate[pl.ds(pl.multiple_of(me * HALF, HALF), HALF), :]
        rows_out[...] = dot3(dot3(mine_rows, factor[...]), block[...])
        a_copy().start()

    root[...] = dot3(iterate[...], factor[...])


    local[2].wait()
    local[3].wait()

    def products(i):
        band = weight[i].reshape(1024, 1024)
        here = jnp.dot(tok_own[:, 1024 * i : 1024 * i + 1024], band, preferred_element_type=jnp.float32)
        if i != 1:
            here = here + projected_sum[...]
        if i != 3:
            projected_sum[...] = here
        else:
            projected[...] = here.astype(jnp.bfloat16)
        input_grad[:, 1024 * i : 1024 * i + 1024] = lax.dot_general(
            ups_own[...], band, (((1,), (1,)), ((), ())), preferred_element_type=jnp.float32
        ).astype(jnp.bfloat16)

    def e_copy(d):
        return remote(energies.at[0], energies.at[d], e_send.at[d], e_recv.at[d], lax.rem(me + d, 8), fs)

    def s_copy(d):
        to = lax.rem(group + d, NB)
        return remote(chunks.at[to], spread.at[group], s_send.at[d], s_recv.at[d], me, 2 * to + 1)

    def n_copy(d):
        return remote(
            norms.at[group], norms.at[group], n_send.at[d], n_recv.at[group], me, lax.rem(fs + d, 32)
        )

    def out_rows(i, q):
        return raw.at[pl.ds(pl.multiple_of(HALF * i + 16 * q, 16), 16)]

    def p_copy(dp, fsdp, b):
        return remote(
            picked.at[b], out_rows(me % 2, my_quarter), p_send.at[b],
            p_recv.at[4 * (me % 2) + my_quarter], dp, fsdp,
        )

    def holder_of(b):
        holder = jnp.int32(0)
        for g in range(1, NB):
            holder = jnp.maximum(holder, jnp.where(table[g] == b, g, 0))
        return holder

    def p_home(b):
        return pltpu.make_async_copy(picked.at[b], out_rows(me % 2, my_quarter), own.at[7])

    @pl.when(side == 1)
    def _():
        a_copy().wait_recv()
        product = dot3(rows_in[...], root[...])
        energies[0] = jnp.full((8, 128), jnp.sum(product * product), jnp.float32)
        for d in (4, 5, 2, 3, 6, 7, 1):
            e_copy(d).start()
        for j in range(NB):
            q, c = j // 4, j % 4
            chunks[j] = product[16 * q : 16 * q + 16, 128 * c : 128 * c + 128]
        for d in (8, 7, 9, 6, 10, 5, 11, 4, 12, 3, 13, 2, 14, 1, 15):
            s_copy(d).start()
        spread[group] = chunks[group]

    for d in (1, 3):
        wf(d, half_from(d, to_y(2))).wait_recv()
    wc(2, rows_from(2, core)).start()
    for d in (1, 3):
        wf(d, half_from(d, y)).wait_send()
        wy(d, 1, y).start()

    @pl.when(side == 1)
    def _():
        for d in range(1, 8):
            e_copy(d).wait_recv()
        total = jnp.zeros((8, 128), jnp.float32)
        for dp in range(8):
            total = total + energies[lax.rem(me - dp + 8, 8)]
        norms[group] = total
        for d in range(1, 32):
            n_copy(d).start()


    @pl.when(side == 1)
    def _():
        for d in range(1, NB):
            source = lax.rem(group + NB - d, NB)
            remote(
                chunks.at[0], spread.at[source], s_send.at[d], s_recv.at[d], me, 2 * source + 1
            ).wait_recv()
        for dp, fsdp, b in places:
            picked[b] = spread[holder_of(b)]

            @pl.when(away(dp, fsdp))
            def _(dp=dp, fsdp=fsdp, b=b):
                p_copy(dp, fsdp, b).start()

            @pl.when(jnp.logical_not(away(dp, fsdp)))
            def _(b=b):
                p_home(b).start()

    wc(0, rows_from(0, 1 - core)).wait()
    wc(2, rows_from(2, 1 - core)).wait()
    for d in (1, 3):
        wc(d, early_part(d, 1 - core)).wait()
    products(1)
    products(2)
    for d in (1, 3):
        wy_from(d, 1).wait_recv()
        wc(d + 3, late_part(d, core)).start()
    for d in (1, 3):
        wc(d + 3, late_part(d, 1 - core)).wait()
    products(0)
    products(3)

    for dp, fsdp, i, q in sources:
        @pl.when(away(dp, fsdp))
        def _(dp=dp, fsdp=fsdp, i=i, q=q):
            remote(picked.at[0], out_rows(i, q), p_send.at[0], p_recv.at[4 * i + q], dp, fsdp).wait_recv()

    for g in range(NB):
        @pl.when(fs != 2 * g + 1)
        def _(g=g):
            remote(norms.at[g], norms.at[g], n_send.at[1], n_recv.at[g], me, mate).wait_recv()

    @pl.when(side == 1)
    def _():
        for dp, fsdp, b in places:
            @pl.when(jnp.logical_not(away(dp, fsdp)))
            def _(b=b):
                p_home(b).wait()

    here = 2 * (fs // 4) + me // 4
    mean = norms[holder_of(here)][0:1, 0:1] / (BS * BS)
    out[...] = (raw[...] / jnp.sqrt(mean + NORM_EPSILON)).astype(jnp.bfloat16)

    @pl.when(side == 0)
    def _():
        a_copy().wait_send()

    @pl.when(side == 1)
    def _():
        for d in range(1, 8):
            e_copy(d).wait_send()
        for d in range(1, NB):
            s_copy(d).wait_send()
        for dp, fsdp, b in places:
            @pl.when(away(dp, fsdp))
            def _(dp=dp, fsdp=fsdp, b=b):
                p_copy(dp, fsdp, b).wait_send()
        for d in range(1, 32):
            n_copy(d).wait_send()

    for d in range(1, 4):
        whole(t_send.at[d], t_recv.at[d], me).wait_send()
        wxa(d).wait_send()
        wxb(d).wait_send()
    for d in range(4):
        whole(f_send.at[d], f_recv.at[d], me).wait_send()
    for d in range(1, 8):
        wza(d).wait_send()
        wzb(d).wait_send()
    for h in range(2):
        for i in range(2):
            xr(h, i).wait_send()
            xd(h, i).wait_send()
            xa(h, i).wait_send()
        for d in range(1, 4):
            xb(h, d).wait_send()
        for d in range(1, 8):
            za(h, d).wait_send()
            zb(h, d).wait_send()
        for d, flip in order:
            g_copy(h, d, flip, mine(h)).wait_send()
    for d in (1, 3):
        wy(d, 0, y).wait_send()
        wy(d, 1, y).wait_send()


def update(table, tokens, upstream, shard, stats_prev, root_prev):
    dma = pltpu.SemaphoreType.DMA
    f32, b16 = jnp.float32, jnp.bfloat16
    anywhere, vmem = pl.BlockSpec(memory_space=pltpu.HBM), pl.BlockSpec(memory_space=pltpu.VMEM)
    rows = tokens.shape[0]
    square = pltpu.VMEM((BS, BS), f32)
    return pl.pallas_call(
        update_kernel,
        out_shape=(
            pltpu.VMEM((rows, 1024), b16),
            pltpu.VMEM((rows, 4096), b16),
            pltpu.VMEM((BS, BS), f32),
            pltpu.VMEM((128, 128), b16),
        ),
        in_specs=[pl.BlockSpec(memory_space=pltpu.SMEM)] + [anywhere] * 5,
        out_specs=(vmem,) * 4,
        scratch_shapes=[
            square,
            pltpu.VMEM((NX, NZ, 128, 1024), b16),
            pltpu.VMEM((rows, 4096), b16),
            pltpu.VMEM((rows, 1024), b16),
        ]
        + [square] * 7
        + [
            pltpu.VMEM((rows, 1024), f32),
            pltpu.VMEM((HALF, BS), f32),
            pltpu.VMEM((HALF, BS), f32),
            pltpu.VMEM((8, 8, 128), f32),
            pltpu.VMEM((NB, 8, 128), f32),
            pltpu.VMEM((NB, 16, 128), f32),
            pltpu.VMEM((NB, 16, 128), f32),
            pltpu.VMEM((NB, 16, 128), f32),
            pltpu.VMEM((128, 128), f32),
            pltpu.VMEM((8, rows, 1024), b16),
            pltpu.VMEM((1024, 8 * rows), b16),
            pltpu.VMEM((2, 8, rows, COLS), b16),
            pltpu.VMEM((2, 8, ROWS, COLS), f32),
            pltpu.VMEM((2, NX, NZ, HALF, 128), f32),
            pltpu.VMEM((2, 2, 4, RA, 128), f32),
            pltpu.VMEM((2, 2, 4, RA, 128), f32),
            pltpu.VMEM((2, 2, NZ, RA, 128), f32),
            pltpu.VMEM((2, NZ, RA, 128), f32),
            pltpu.VMEM((2, NZ, RA, 128), f32),
            pltpu.VMEM((2, NZ, NX, HALF - RA, 128), f32),
            pltpu.VMEM((2, NX, HALF - RA, 128), f32),
            pltpu.VMEM((2, NX, HALF - RA, 128), f32),
        ]
        + [dma((4,))] * 4
        + [dma((2, 8))] * 2
        + [dma((2, 2))] * 6
        + [dma((2, 8))] * 4
        + [dma((2, 4))] * 2
        + [dma((2, 8))] * 4
        + [dma((8,))] * 2
        + [dma((4,))] * 2
        + [dma((8,))] * 2
        + [dma((4,))] * 2
        + [dma((2, 4))] * 2
        + [dma((4,))] * 2
        + [dma((8,))] * 2
        + [dma((9,)), dma(()), dma(()), dma((8,)), dma((8,)), dma((32,)), dma((NB,))]
        + [dma((NB,))] * 3
        + [dma((8,))],
        compiler_params=pltpu.CompilerParams(
            collective_id=0, has_side_effects=True, vmem_limit_bytes=VMEM_LIMIT
        ),
        cost_estimate=pl.CostEstimate(flops=0, bytes_accessed=64 << 20, transcendentals=0),
    )(
        *(
            pltpu.with_memory_space_constraint(a, pltpu.HBM)
            for a in (table, tokens, upstream, shard, stats_prev, root_prev)
        )
    )


def settle_kernel(*refs):
    n = len(refs) // 2
    copies = [pltpu.make_async_copy(refs[i], refs[n + i], refs[-1].at[i]) for i in range(n)]
    for copy in copies:
        copy.start()
    for copy in copies:
        copy.wait()


def settle(*arrays):
    n = len(arrays)
    return pl.pallas_call(
        settle_kernel,
        out_shape=tuple(pltpu.HBM(a.shape, a.dtype) for a in arrays),
        in_specs=[pl.BlockSpec(memory_space=pltpu.VMEM)] * n,
        out_specs=(pl.BlockSpec(memory_space=pltpu.HBM),) * n,
        scratch_shapes=[pltpu.SemaphoreType.DMA((n,))],
        compiler_params=pltpu.CompilerParams(vmem_limit_bytes=16 * 1024 * 1024),
    )(*(pltpu.with_memory_space_constraint(a, pltpu.VMEM) for a in arrays))


def local(tokens, upstream, weight, owner_table, stats_prev, roots_prev):
    projected, input_grad, root, direction = settle(
        *update(owner_table, tokens, upstream, weight, stats_prev[0], roots_prev[0])
    )
    return projected, input_grad, root[None], direction


def solution(mesh):
    placed = (
        P(("dp", "fsdp"), None),
        P(("dp", "fsdp"), None),
        P("fsdp", None),
        P(),
        P("fsdp", None, None),
        P("fsdp", None, None),
    )
    return jax.shard_map(
        local,
        mesh=mesh,
        in_specs=placed,
        out_specs=(
            P(("dp", "fsdp"), None),
            P(("dp", "fsdp"), None),
            P("fsdp", None, None),
            P("fsdp", "dp"),
        ),
        check_vma=False,
    )
```
